256 devices in a mesh: blk: 32 (over y, z_hi, x), head: 8 (over z_lo, core).
Axes of the slice: x: 4, y: 4, z: 8 (z_hi: 2, z_lo: 4; z = z_hi * 4 + z_lo), core: 2. Of those that a mesh axis runs over, the one named last changes fastest.
Arguments:
- queries: bfloat16 [4096, 3072], P(('blk', 'head')), may hold values from -32 to 32
- key_vectors: bfloat16 [4096, 3072], P(('blk', 'head')), may hold values from -9 to 9
- values: bfloat16 [4096, 3072], P(('blk', 'head')), may hold values from -6 to 6
- query_tangent: bfloat16 [4096, 3072], P(('blk', 'head')), may hold values from -6 to 6
- key_tangent: bfloat16 [4096, 3072], P(('blk', 'head')), may hold values from -6 to 6
- value_tangent: bfloat16 [4096, 3072], P(('blk', 'head')), may hold values from -6 to 6
- frame_index: int32 [4096], P('blk'), may hold values from 0 to 20, as said below
- valid_counts: int32 [32], P('blk'), may hold values from 32 to 128, as said below
Outputs:
- attended: bfloat16 [4096, 3072], P(('blk', 'head'))
- attended_tangent: bfloat16 [4096, 3072], P(('blk', 'head'))
The draws below stay inside these ranges and needn't reach their ends.
Inputs may be any that keep to these rules, and one draw needn't show every extreme that they name: `frame_index`: never falls from one token to the next. `valid_counts`: every key block but the last is full (128 valid keys); the last holds at least 32.
All inputs are finite; a program needn't handle non-finite values.
Results may differ from the reference program's by a relative error of at most 0.033.
Values may be sent and summed in bfloat16 or wider, within the bound.
A program may use at most 128 MiB of HBM per device.

```python
import math
import jax
import jax.numpy as jnp
from jax import lax

HD = 128
HEADS = 24
ROWS = 128
TOKENS = 4096
GROUPS = 32
FRAME_TOKENS = 3600
GRID_WIDTH = 80


def shared_keys(key):
    return jax.random.normal(key, (TOKENS, HEADS * HD), jnp.float32)


def key_scale():
    return 1.5


def draw_key_vectors(key, part):
    shared_base = shared_keys(key)
    return jnp.clip(key_scale() * shared_base, -9.0, 9.0).astype(jnp.bfloat16)


def draw_queries(key, part):
    key = jax.random.fold_in(key, 5)
    own_noise = jax.random.normal(key, (TOKENS, HEADS * HD), jnp.float32)
    return jnp.clip(2.0 * own_noise, -12.0, 12.0).astype(jnp.bfloat16)


def draw_frame_index(key, part):
    key = jax.random.fold_in(key, 3)
    jumps = (jax.random.randint(key, (TOKENS,), 0, max(TOKENS // 6, 2)) == 0).astype(jnp.int32)
    total_jumps = jnp.sum(jumps)
    later_jumps = total_jumps - jnp.cumsum(jumps)
    return jnp.maximum(20 - later_jumps, 0).astype(jnp.int32)


def draw_valid_counts(key, part):
    key = jax.random.fold_in(key, 9)
    last_count = jax.random.randint(key, (1,), ROWS // 4, ROWS + 1)
    full_counts = jnp.full((GROUPS - 1,), ROWS, jnp.int32)
    return jnp.concatenate([full_counts, last_count.astype(jnp.int32)]).astype(jnp.int32)


def shard_levels(key, dims, pieces, low, high):
    def one(dim, blocks):
        draws = jax.random.uniform(jax.random.fold_in(jax.random.fold_in(key, 6), dim), (blocks,), jnp.float32, low / len(pieces), high / len(pieces))
        return jnp.repeat(jnp.exp(draws), dims[dim] // blocks).reshape((-1,) + (1,) * (len(dims) - dim - 1))

    level = one(*pieces[0])
    for cut in pieces[1:]:
        level = level * one(*cut)
    return level


def centred(stream_key, extent, scale, bound, cuts=(), kind=jnp.bfloat16):
    factor_of = shard_levels(stream_key, extent, cuts, -0.22, 0.18) if cuts else 1.0
    values = jax.random.normal(stream_key, extent, jnp.float32) * scale * factor_of
    return jnp.minimum(jnp.maximum(values, -bound), bound).astype(kind)


def setup_inputs(seed: int = 0) -> dict:
    splits = jax.random.split(jax.random.key(seed), 9)
    return {
        "queries": draw_queries(jax.random.fold_in(splits[8], 71), 0),
        "key_vectors": draw_key_vectors(jax.random.fold_in(splits[8], 71), 0),
        "values": centred(splits[2], (TOKENS, HEADS * HD), 1.0, 6.0, ((0, 256),)),
        "query_tangent": centred(splits[3], (TOKENS, HEADS * HD), 1.0, 6.0, ((0, 256),)),
        "key_tangent": centred(splits[4], (TOKENS, HEADS * HD), 1.0, 6.0, ((0, 256),)),
        "value_tangent": centred(splits[5], (TOKENS, HEADS * HD), 1.0, 6.0, ((0, 256),)),
        "frame_index": draw_frame_index(jax.random.fold_in(splits[8], 71), 0),
        "valid_counts": draw_valid_counts(jax.random.fold_in(splits[8], 71), 0),
    }


def part_freqs(pair_count):
    indices = jnp.arange(pair_count, dtype=jnp.float32)
    return jnp.exp(-math.log(10000.0) * indices / pair_count)

def rotation(frames, token_ids):
    temporal = HD // 2 - 2 * (HD // 6)
    spatial = HD // 6
    height = (token_ids % FRAME_TOKENS // GRID_WIDTH).astype(jnp.float32)
    across = (token_ids % GRID_WIDTH).astype(jnp.float32)
    angles = jnp.concatenate([frames.astype(jnp.float32)[:, None] * part_freqs(temporal)[None, :], height[:, None] * part_freqs(spatial)[None, :], across[:, None] * part_freqs(spatial)[None, :]], axis=1)
    cosine_table = jnp.cos(angles)
    sine_table = jnp.sin(angles)
    return (jnp.concatenate([cosine_table, cosine_table], axis=1), jnp.concatenate([-sine_table, sine_table], axis=1))

def rotate(tensor, cosine_table, sine_table):
    widened = tensor.astype(jnp.float32)
    half_dim = HD // 2
    swapped = jnp.concatenate([widened[..., half_dim:], widened[..., :half_dim]], axis=-1)
    return (widened * cosine_table[:, None, :] + swapped * sine_table[:, None, :]).astype(jnp.bfloat16)

def reference(queries, key_vectors, values, query_tangent, key_tangent, value_tangent, frame_index, valid_counts):
    token_ids = jnp.arange(TOKENS, dtype=jnp.int32)
    cosine_table, sine_table = rotation(frame_index, token_ids)

    def split_heads(tensor):
        return tensor.reshape(TOKENS, HEADS, HD)
    query_rot = rotate(split_heads(queries), cosine_table, sine_table)
    key_rot = rotate(split_heads(key_vectors), cosine_table, sine_table)
    qtan_rot = rotate(split_heads(query_tangent), cosine_table, sine_table)
    ktan_rot = rotate(split_heads(key_tangent), cosine_table, sine_table)
    group_of = (token_ids // ROWS).astype(jnp.int32)
    valid_keys = token_ids % ROWS < valid_counts[group_of]
    score_scale = 1.0 / math.sqrt(HD)

    def head_attention(operands):
        query_head, key_head, value_head, qtan_head, ktan_head, vtan_head = operands
        raw_scores = jnp.dot(query_head, key_head.T, preferred_element_type=jnp.float32) * score_scale
        scores = jnp.where(valid_keys[None, :], raw_scores, -jnp.inf)
        slopes = (jnp.dot(qtan_head, key_head.T, preferred_element_type=jnp.float32) + jnp.dot(query_head, ktan_head.T, preferred_element_type=jnp.float32)) * score_scale
        weights = jax.nn.softmax(scores, axis=1)
        weighted = weights * slopes
        weights_low = weights.astype(jnp.bfloat16)
        weighted_low = weighted.astype(jnp.bfloat16)
        attended_full = jnp.dot(weights_low, value_head, preferred_element_type=jnp.float32)
        mean_slope = lax.optimization_barrier(jnp.sum(weighted, axis=1))
        tangent_full = jnp.dot(weighted_low, value_head, preferred_element_type=jnp.float32) + jnp.dot(weights_low, vtan_head, preferred_element_type=jnp.float32) - mean_slope[:, None] * attended_full
        return (attended_full.astype(jnp.bfloat16), tangent_full.astype(jnp.bfloat16))
    stacked = tuple((jnp.transpose(member, (1, 0, 2)) for member in (query_rot, key_rot, split_heads(values), qtan_rot, ktan_rot, split_heads(value_tangent))))
    attended_heads, tangent_heads = lax.map(head_attention, stacked)
    attended = jnp.transpose(attended_heads, (1, 0, 2)).reshape(TOKENS, HEADS * HD)
    attended_tangent = jnp.transpose(tangent_heads, (1, 0, 2)).reshape(TOKENS, HEADS * HD)
    return (attended, attended_tangent)
```

```python
import math

import jax
import jax.numpy as jnp
from jax import lax
from jax.experimental import pallas as pl
from jax.experimental.pallas import tpu as pltpu
from jax.sharding import PartitionSpec as P

HD = 128
FRAME_TOKENS = 3600
GRID_WIDTH = 80
ROWS = 16

X, Y, ZH, ZL, C = 4, 4, 2, 4, 2
J = 3

MARK = 16384.0
MARK_SUM = 1.0e5
LOW = -1.0e30

K, KT, Q, QT, V, VT = range(6)
GROUPS = ((0, 1), (1, 3), (4, 2))
RING = (K, KT, V, VT)


def part_freqs(pair_count):
    indices = jnp.arange(pair_count, dtype=jnp.float32)
    return jnp.exp(-math.log(10000.0) * indices / pair_count)


def rotation(frames, token_ids):
    temporal = HD // 2 - 2 * (HD // 6)
    spatial = HD // 6
    height = (token_ids % FRAME_TOKENS // GRID_WIDTH).astype(jnp.float32)
    across = (token_ids % GRID_WIDTH).astype(jnp.float32)
    angles = jnp.concatenate(
        [
            frames.astype(jnp.float32)[:, None] * part_freqs(temporal)[None, :],
            height[:, None] * part_freqs(spatial)[None, :],
            across[:, None] * part_freqs(spatial)[None, :],
        ],
        axis=1,
    )
    cosine_table = jnp.cos(angles)
    sine_table = jnp.sin(angles)
    return (
        jnp.concatenate([cosine_table, cosine_table], axis=1),
        jnp.concatenate([-sine_table, sine_table], axis=1),
    )


def device(x, y, z, c):
    return (y * (ZH * X) + lax.div(z, ZL) * X + x, lax.rem(z, ZL) * C + c)


def nt_dot(a, b):
    return lax.dot_general(a, b, (((1,), (1,)), ((), ())), preferred_element_type=jnp.float32)


def nn_dot(a, b):
    return jnp.dot(a, b, preferred_element_type=jnp.float32)


def kernel(
    q_ref, k_ref, v_ref, qt_ref, kt_ref, vt_ref, cos_ref, sin_ref, valid_ref,
    o_ref, ot_ref,
    send, kv, s_ref, p_ref, w_ref, acc_p, acc_w, mx, lsum, gsum, outsend, outland,
    dsem, rsem, ssem, dsend, rsend, bsend, osem, osend,
):
    Z = ZH * ZL
    heads = Z * J
    span = Z * ROWS
    chunks = X * C
    half = Y // 2
    keys = Y * span
    scale = 1.0 / math.sqrt(HD)
    scale2 = scale * math.log2(math.e)

    blk = lax.axis_index("blk")
    hd = lax.axis_index("head")
    x = lax.rem(blk, X)
    y = lax.div(blk, ZH * X)
    z = lax.rem(lax.div(blk, X), ZH) * ZL + lax.div(hd, C)
    c = lax.rem(hd, C)
    right = device(lax.rem(x + 1, X), y, z, c)
    left = device(lax.rem(x + X - 1, X), y, z, c)
    sib = device(x, y, z, 1 - c)
    own = (x * C + c) * Y
    computes = y < J

    barrier = pltpu.get_barrier_semaphore()

    def greet(i, carry):
        gy = lax.div(i, Z)
        gz = lax.rem(i, Z)

        @pl.when(jnp.logical_or(gy != y, gz != z))
        def _():
            pl.semaphore_signal(barrier, inc=1, device_id=device(x, gy, gz, c))

        return carry

    lax.fori_loop(0, Y * Z, greet, 0)
    for other in (right, left, sib):
        pl.semaphore_signal(barrier, inc=1, device_id=other)

    cosine = cos_ref[...]
    sine = sin_ref[...]
    valid = valid_ref[...] > 0.0

    def rotate(ref, slot, marked):
        for h in range(heads):
            wide = ref[:, h * HD : (h + 1) * HD].astype(jnp.float32)
            turned = wide * cosine + pltpu.roll(wide, HD // 2, 1) * sine
            if marked:
                turned = jnp.where(valid, turned, MARK)
            send[h, slot] = turned.astype(jnp.bfloat16)

    def place(ref, slot):
        for h in range(heads):
            send[h, slot] = ref[:, h * HD : (h + 1) * HD]

    def direct(g):
        first, count = GROUPS[g]

        def step(i, carry):
            m = lax.div(i + 1, 2)
            tz = lax.rem(z + jnp.where(lax.rem(i, 2) == 1, m, Z - m), Z)
            for j in range(J):
                src = send.at[tz * J + j, pl.ds(first, count)]
                dst = kv.at[pl.ds(first, count), own + y, pl.ds(z * ROWS, ROWS)]
                here = jnp.logical_and(tz == z, y == j)

                @pl.when(here)
                def _():
                    pltpu.make_async_copy(src, dst, dsem.at[g]).start()

                @pl.when(jnp.logical_not(here))
                def _():
                    pltpu.make_async_remote_copy(
                        src_ref=src, dst_ref=dst, send_sem=dsend.at[g], recv_sem=dsem.at[g],
                        device_id=device(x, j, tz, c),
                    ).start()

            return carry

        lax.fori_loop(0, Z, step, 0)

    def wait_direct(g):
        first, count = GROUPS[g]
        region = kv.at[pl.ds(first, count), pl.ds(own, Y)]
        pltpu.make_async_copy(region, region, dsem.at[g]).wait()

    def region(a, sx, sc, u):
        return kv.at[a, pl.ds((sx * C + sc) * Y + u * half, half)]

    def ring_send(a, part, to, event):
        n = RING.index(a)
        pltpu.make_async_remote_copy(
            src_ref=part, dst_ref=part, send_sem=rsend.at[n], recv_sem=rsem.at[n, event],
            device_id=to,
        ).start()

    def sib_send(a, part):
        n = RING.index(a)
        pltpu.make_async_remote_copy(
            src_ref=part, dst_ref=part, send_sem=bsend.at[n], recv_sem=ssem.at[n],
            device_id=sib,
        ).start()

    def start_own(a):
        first, second = region(a, x, c, 0), region(a, x, c, 1)
        ring_send(a, first, right, 2)
        ring_send(a, second, left, 3)
        ring_send(a, second, right, 4)
        ring_send(a, first, left, 5)
        sib_send(a, first)
        sib_send(a, second)

    def event(a, i):
        n = RING.index(a)
        far = jnp.where(i >= 6, 2, 1)
        from_left = lax.rem(i, 2) == 0
        sx = lax.rem(jnp.where(from_left, x + X - far, x + far), X)
        u = jnp.where(from_left, jnp.where(i == 4, 1, 0), jnp.where(i == 5, 0, 1))
        part = region(a, sx, c, u)
        pltpu.make_async_copy(part, part, rsem.at[n, i]).wait()

        @pl.when(i == 2)
        def _():
            ring_send(a, part, right, 6)

        @pl.when(i == 3)
        def _():
            ring_send(a, part, left, 7)

        sib_send(a, part)

    def wait_sib(a):
        part = kv.at[a, pl.ds(0, chunks * Y // 2)]
        pltpu.make_async_copy(part, part, ssem.at[RING.index(a)]).wait()

    def queries_of(a):
        return kv[a, pl.ds(own, Y)].reshape(keys, HD)

    def chunk(a, i):
        return kv[a, pl.ds(i * Y, Y)].reshape(keys, HD)

    def lanes(op, total, array):
        for t in range(array.shape[1] // HD):
            total = op(total, array[:, t * HD : (t + 1) * HD])
        return total

    def scores(i):
        s = nt_dot(queries_of(Q), chunk(K, i))
        tail = keys - span
        marks = nt_dot(jnp.ones((8, HD), jnp.bfloat16), kv[K, i * Y + Y - 1])[0:1]
        last = jnp.where(marks > MARK_SUM, LOW, s[:, tail:])
        s = jnp.concatenate([s[:, :tail], last], axis=1)
        s_ref[i] = s
        mx[...] = lanes(jnp.maximum, mx[...], s)

    def weights(i):
        top = jnp.concatenate([mx[...]] * (keys // HD), axis=1)
        p = jnp.exp2(s_ref[i] * scale2 - top)
        g = nt_dot(
            jnp.concatenate([queries_of(QT), queries_of(Q)], axis=1),
            jnp.concatenate([chunk(K, i), chunk(KT, i)], axis=1),
        )
        w = p * g
        lsum[...] = lanes(jnp.add, lsum[...], p)
        gsum[...] = lanes(jnp.add, gsum[...], w)
        p_ref[i] = p.astype(jnp.bfloat16)
        w_ref[i] = w.astype(jnp.bfloat16)

    def slope_values(i):
        acc_w[...] += nn_dot(w_ref[i], chunk(V, i))

    def weight_values(i):
        acc_p[...] += nn_dot(p_ref[i], jnp.concatenate([chunk(V, i), chunk(VT, i)], axis=1))

    rotate(k_ref, K, True)
    pl.semaphore_wait(barrier, Y * Z - 1 + 3)
    direct(0)
    rotate(kt_ref, KT, False)
    rotate(q_ref, Q, False)
    rotate(qt_ref, QT, False)
    direct(1)
    place(v_ref, V)
    place(vt_ref, VT)
    direct(2)

    @pl.when(computes)
    def _():
        mx[...] = jnp.full_like(mx, LOW)
        lsum[...] = jnp.zeros_like(lsum)
        gsum[...] = jnp.zeros_like(gsum)
        acc_p[...] = jnp.zeros_like(acc_p)
        acc_w[...] = jnp.zeros_like(acc_w)

        def phase(a, work, following):
            def step(i, carry):
                @pl.when(i >= 2)
                def _():
                    event(a, i)

                if following is not None:

                    @pl.when(i == 4)
                    def _():
                        following()

                if work is not None:
                    work(i)
                return carry

            lax.fori_loop(0, 8, step, 0)
            wait_sib(a)

        def begin(g, a):
            wait_direct(g)
            start_own(a)

        begin(0, K)
        phase(K, None, lambda: begin(1, KT))
        phase(KT, scores, lambda: begin(2, V))
        mx[...] = jnp.broadcast_to(
            jnp.max(mx[...], axis=1, keepdims=True) * scale2, mx.shape
        )
        phase(V, weights, lambda: start_own(VT))
        phase(VT, slope_values, None)

        def tail(i, carry):
            weight_values(i)
            return carry

        lax.fori_loop(0, chunks, tail, 0)

        inverse = 1.0 / jnp.sum(lsum[...], axis=1, keepdims=True)
        slope = jnp.sum(gsum[...], axis=1, keepdims=True) * inverse * scale
        attended = acc_p[:, :HD] * inverse
        tangent = (acc_w[...] * scale + acc_p[:, HD:]) * inverse - slope * attended
        outsend[:, 0] = attended.astype(jnp.bfloat16).reshape(Y * Z, ROWS, HD)
        outsend[:, 1] = tangent.astype(jnp.bfloat16).reshape(Y * Z, ROWS, HD)

        def give(i, carry):
            m = lax.div(i + 1, 2)
            tz = lax.rem(z + jnp.where(lax.rem(i, 2) == 1, m, Z - m), Z)
            for ty in range(Y):
                src = outsend.at[ty * Z + tz]
                dst = outland.at[z * J + y]
                here = jnp.logical_and(tz == z, y == ty)

                @pl.when(here)
                def _():
                    pltpu.make_async_copy(src, dst, osem).start()

                @pl.when(jnp.logical_not(here))
                def _():
                    pltpu.make_async_remote_copy(
                        src_ref=src, dst_ref=dst, send_sem=osend, recv_sem=osem,
                        device_id=device(x, ty, tz, c),
                    ).start()

            return carry

        lax.fori_loop(0, Z, give, 0)

    pltpu.make_async_copy(outland, outland, osem).wait()
    for h in range(heads):
        o_ref[:, h * HD : (h + 1) * HD] = outland[h, 0]
        ot_ref[:, h * HD : (h + 1) * HD] = outland[h, 1]

    def sent(g, count):
        first, arrays = GROUPS[g]
        part = send.at[pl.ds(0, count), pl.ds(first, arrays)]
        pltpu.make_async_copy(part, part, dsend.at[g]).wait()

    @pl.when(computes)
    def _():
        for g in range(3):
            sent(g, heads - 1)
        for n in range(4):
            part = kv.at[0, pl.ds(0, 6 * half)]
            pltpu.make_async_copy(part, part, rsend.at[n]).wait()
            part = kv.at[0, pl.ds(0, 8 * half)]
            pltpu.make_async_copy(part, part, bsend.at[n]).wait()
        part = outsend.at[pl.ds(0, Y * Z - 1)]
        pltpu.make_async_copy(part, part, osend).wait()

    @pl.when(jnp.logical_not(computes))
    def _():
        for g in range(3):
            sent(g, heads)


def shards(queries, key_vectors, values, query_tangent, key_tangent, value_tangent,
           frame_index, valid_counts):
    Z = ZH * ZL
    heads = Z * J
    span = Z * ROWS
    rows = Y * span
    chunks = X * C
    blk = lax.axis_index("blk")
    hd = lax.axis_index("head")
    inner = hd * ROWS + jnp.arange(ROWS, dtype=jnp.int32)
    token_ids = blk * (ROWS * ZL * C) + inner
    frames = lax.dynamic_slice(frame_index, (hd * ROWS,), (ROWS,))
    cosine_table, sine_table = rotation(frames, token_ids)
    valid = jnp.broadcast_to((inner < valid_counts[0]).astype(jnp.float32)[:, None], (ROWS, HD))

    vmem = pl.BlockSpec(memory_space=pltpu.VMEM)
    out = jax.ShapeDtypeStruct((ROWS, heads * HD), jnp.bfloat16)
    return pl.pallas_call(
        kernel,
        out_shape=(out, out),
        in_specs=[vmem] * 9,
        out_specs=(vmem, vmem),
        scratch_shapes=[
            pltpu.VMEM((heads, 6, ROWS, HD), jnp.bfloat16),
            pltpu.VMEM((6, chunks * Y, span, HD), jnp.bfloat16),
            pltpu.VMEM((chunks, rows, rows), jnp.float32),
            pltpu.VMEM((chunks, rows, rows), jnp.bfloat16),
            pltpu.VMEM((chunks, rows, rows), jnp.bfloat16),
            pltpu.VMEM((rows, 2 * HD), jnp.float32),
            pltpu.VMEM((rows, HD), jnp.float32),
            pltpu.VMEM((rows, HD), jnp.float32),
            pltpu.VMEM((rows, HD), jnp.float32),
            pltpu.VMEM((rows, HD), jnp.float32),
            pltpu.VMEM((Y * Z, 2, ROWS, HD), jnp.bfloat16),
            pltpu.VMEM((heads, 2, ROWS, HD), jnp.bfloat16),
            pltpu.SemaphoreType.DMA((3,)),
            pltpu.SemaphoreType.DMA((4, 8)),
            pltpu.SemaphoreType.DMA((4,)),
            pltpu.SemaphoreType.DMA((3,)),
            pltpu.SemaphoreType.DMA((4,)),
            pltpu.SemaphoreType.DMA((4,)),
            pltpu.SemaphoreType.DMA,
            pltpu.SemaphoreType.DMA,
        ],
        compiler_params=pltpu.CompilerParams(
            collective_id=0, has_side_effects=True, vmem_limit_bytes=52 * 1024 * 1024
        ),
    )(queries, key_vectors, values, query_tangent, key_tangent, value_tangent,
      cosine_table, sine_table, valid)


def solution(mesh):
    tokens = P(("blk", "head"), None)
    return jax.shard_map(
        shards,
        mesh=mesh,
        in_specs=(tokens,) * 6 + (P("blk"), P("blk")),
        out_specs=(tokens, tokens),
        check_vma=False,
    )
```

```python
import math

import jax
import jax.numpy as jnp
from jax import lax
from jax.experimental import pallas as pl
from jax.experimental.pallas import tpu as pltpu
from jax.sharding import PartitionSpec as P

HD = 128
FRAME_TOKENS = 3600
GRID_WIDTH = 80
ROWS = 16

X, Y, ZH, ZL, C = 4, 4, 2, 4, 2
J = 3

MARK = 16384.0
MARK_SUM = 1.0e5
LOW = -1.0e30

K, KT, Q, QT, V, VT = range(6)
GROUPS = ((K, 1), (KT, 1), (Q, 2), (V, 1), (VT, 1))
RING = (K, KT, V, VT)


def device(x, y, z, c):
    return (y * (ZH * X) + lax.div(z, ZL) * X + x, lax.rem(z, ZL) * C + c)


def nt_dot(a, b):
    return lax.dot_general(a, b, (((1,), (1,)), ((), ())), preferred_element_type=jnp.float32)


def nn_dot(a, b):
    return jnp.dot(a, b, preferred_element_type=jnp.float32)


def kernel(
    q_in, k_in, v_in, qt_in, kt_in, vt_in, frame_ref, count_ref,
    o_out, ot_out,
    raw, send, kv, s_ref, p_ref, w_ref, acc_p, acc_w, acc_t, mx, lsum, gsum, outsend, outland, final,
    isem, dsem, rsem, ssem, dsend, rsend, bsend, osem, osend, fsem,
):
    Z = ZH * ZL
    heads = Z * J
    span = Z * ROWS
    chunks = X * C
    half = Y // 2
    keys = Y * span
    scale = 1.0 / math.sqrt(HD)
    scale2 = scale * math.log2(math.e)

    blk = lax.axis_index("blk")
    hd = lax.axis_index("head")
    x = lax.rem(blk, X)
    y = lax.div(blk, ZH * X)
    z = lax.rem(lax.div(blk, X), ZH) * ZL + lax.div(hd, C)
    c = lax.rem(hd, C)
    right = device(lax.rem(x + 1, X), y, z, c)
    left = device(lax.rem(x + X - 1, X), y, z, c)
    sib = device(x, y, z, 1 - c)
    own = (x * C + c) * Y
    computes = y < J

    def fetch(ref, slot):
        return pltpu.make_async_copy(ref, raw.at[slot], isem.at[slot])

    inputs = ((k_in, K), (kt_in, KT), (q_in, Q), (qt_in, QT), (v_in, V), (vt_in, VT))
    for ref, slot in inputs:
        fetch(ref, slot).start()

    barrier = pltpu.get_barrier_semaphore()

    def around(i):
        m = lax.div(i + 1, 2)
        return lax.rem(z + jnp.where(lax.rem(i, 2) == 1, m, Z - m), Z)

    def greet(i, carry):
        gz = around(Z - 1 - i)
        for gy in range(Y):

            @pl.when(jnp.logical_or(gy != y, gz != z))
            def _():
                pl.semaphore_signal(barrier, inc=1, device_id=device(x, gy, gz, c))

        return carry

    lax.fori_loop(0, Z, greet, 0)
    for other in (right, left, sib):
        pl.semaphore_signal(barrier, inc=1, device_id=other)

    row = lax.broadcasted_iota(jnp.int32, (ROWS, HD), 0)
    lane = lax.broadcasted_iota(jnp.int32, (ROWS, HD), 1)
    frame = jnp.zeros((ROWS, HD), jnp.float32)
    for i in range(ROWS):
        frame = jnp.where(row == i, frame_ref[hd * ROWS + i].astype(jnp.float32), frame)
    valid = hd * ROWS + row < count_ref[0]
    token = blk * (ROWS * ZL * C) + hd * ROWS + row
    token = jnp.where(token >= FRAME_TOKENS, token - FRAME_TOKENS, token).astype(jnp.float32)
    height = jnp.floor((token + 0.5) * (1.0 / GRID_WIDTH))
    across = token - height * GRID_WIDTH
    pair = lax.rem(lane, HD // 2)
    spatial = HD // 6
    temporal = HD // 2 - 2 * spatial
    is_frame = pair < temporal
    is_height = pair < temporal + spatial
    index = jnp.where(is_frame, pair, jnp.where(is_height, pair - temporal, pair - temporal - spatial))
    count = jnp.where(is_frame, float(temporal), float(spatial))
    freqs = jnp.exp(-math.log(10000.0) * index.astype(jnp.float32) / count)
    angles = jnp.where(is_frame, frame, jnp.where(is_height, height, across)) * freqs
    cosine = jnp.cos(angles)
    sine = jnp.sin(angles)
    sine = jnp.where(lane < HD // 2, -sine, sine)

    def rotate(ref, slot, marked=False):
        fetch(ref, slot).wait()
        for h in range(heads):
            wide = raw[slot, :, h * HD : (h + 1) * HD].astype(jnp.float32)
            turned = wide * cosine + pltpu.roll(wide, HD // 2, 1) * sine
            if marked:
                turned = jnp.where(valid, turned, MARK)
            send[h, slot] = turned.astype(jnp.bfloat16)

    def place(ref, slot):
        fetch(ref, slot).wait()
        for h in range(heads):
            send[h, slot] = raw[slot, :, h * HD : (h + 1) * HD]

    def direct(g):
        first, count = GROUPS[g]

        def step(i, carry):
            tz = around(i)
            for j in range(J):
                src = send.at[tz * J + j, pl.ds(first, count)]
                dst = kv.at[pl.ds(first, count), own + y, pl.ds(z * ROWS, ROWS)]
                here = jnp.logical_and(tz == z, y == j)

                @pl.when(here)
                def _():
                    pltpu.make_async_copy(src, dst, dsem.at[g]).start()

                @pl.when(jnp.logical_not(here))
                def _():
                    pltpu.make_async_remote_copy(
                        src_ref=src, dst_ref=dst, send_sem=dsend.at[g], recv_sem=dsem.at[g],
                        device_id=device(x, j, tz, c),
                    ).start()

            return carry

        lax.fori_loop(0, Z, step, 0)

    def sent(g, count):
        first, arrays = GROUPS[g]
        part = send.at[pl.ds(0, count), pl.ds(first, arrays)]
        pltpu.make_async_copy(part, part, dsend.at[g]).wait()

    def wait_direct(g):
        first, count = GROUPS[g]
        region = kv.at[pl.ds(first, count), pl.ds(own, Y)]
        pltpu.make_async_copy(region, region, dsem.at[g]).wait()

    def region(a, sx, sc, u):
        return kv.at[a, pl.ds((sx * C + sc) * Y + u * half, half)]

    def ring_send(a, part, to, event):
        n = RING.index(a)
        pltpu.make_async_remote_copy(
            src_ref=part, dst_ref=part, send_sem=rsend.at[n], recv_sem=rsem.at[n, event],
            device_id=to,
        ).start()

    def sib_send(a, part, event):
        n = RING.index(a)
        pltpu.make_async_remote_copy(
            src_ref=part, dst_ref=part, send_sem=bsend.at[n], recv_sem=ssem.at[n, event],
            device_id=sib,
        ).start()

    def start_own(a):
        first, second = region(a, x, c, 0), region(a, x, c, 1)
        ring_send(a, first, right, 2)
        ring_send(a, second, left, 3)
        ring_send(a, second, right, 4)
        ring_send(a, first, left, 5)
        sib_send(a, first, 0)
        sib_send(a, second, 1)

    def origin(i):
        far = jnp.where(i >= 6, 2, jnp.where(i >= 2, 1, 0))
        even = lax.rem(i, 2) == 0
        sx = lax.rem(jnp.where(even, x + X - far, x + far), X)
        swap = jnp.logical_or(i == 4, i == 5)
        u = jnp.where(jnp.logical_xor(even, swap), 0, 1)
        return sx, u

    def event(a, i):
        n = RING.index(a)
        sx, u = origin(i)
        part = region(a, sx, c, u)
        pltpu.make_async_copy(part, part, rsem.at[n, i]).wait()

        @pl.when(i == 2)
        def _():
            ring_send(a, part, right, 6)

        @pl.when(i == 3)
        def _():
            ring_send(a, part, left, 7)

        sib_send(a, part, i)

    def events(a, start, stop):
        def step(i, carry):
            event(a, i)
            return carry

        lax.fori_loop(start, stop, step, 0)

    def wait_sib(a, i):
        sx, u = origin(i)
        part = region(a, sx, 1 - c, u)
        pltpu.make_async_copy(part, part, ssem.at[RING.index(a), i]).wait()

    def wait_sibs(a):
        def step(i, carry):
            wait_sib(a, i)
            return carry

        lax.fori_loop(0, 8, step, 0)

    def queries_of(a):
        return kv[a, pl.ds(own, Y)].reshape(keys, HD)

    def chunk(a, i):
        return kv[a, pl.ds(i * Y, Y)].reshape(keys, HD)

    def unit(a, i):
        return kv[a, pl.ds(i * half, half)].reshape(keys // 2, HD)

    def lanes(op, total, array):
        for t in range(array.shape[1] // HD):
            total = op(total, array[:, t * HD : (t + 1) * HD])
        return total

    def scores(i):
        s = nt_dot(queries_of(Q), chunk(K, i))
        tail = keys - span
        marks = nt_dot(jnp.ones((8, HD), jnp.bfloat16), kv[K, i * Y + Y - 1])[0:1]
        last = jnp.where(marks > MARK_SUM, LOW, s[:, tail:])
        s = jnp.concatenate([s[:, :tail], last], axis=1)
        s_ref[i] = s
        mx[...] = lanes(jnp.maximum, mx[...], s)

    def weights(i):
        top = jnp.concatenate([mx[...]] * (keys // HD), axis=1)
        p = jnp.exp2(s_ref[i] * scale2 - top)
        g = nt_dot(
            jnp.concatenate([queries_of(QT), queries_of(Q)], axis=1),
            jnp.concatenate([chunk(K, i), chunk(KT, i)], axis=1),
        )
        w = p * g
        lsum[...] = lanes(jnp.add, lsum[...], p)
        gsum[...] = lanes(jnp.add, gsum[...], w)
        p = p.astype(jnp.bfloat16)
        w = w.astype(jnp.bfloat16)
        for u in range(2):
            p_ref[2 * i + u] = p[:, u * (keys // 2) : (u + 1) * (keys // 2)]
            w_ref[2 * i + u] = w[:, u * (keys // 2) : (u + 1) * (keys // 2)]

    def value_products(i):
        p = jnp.concatenate([p_ref[2 * i], p_ref[2 * i + 1]], axis=1)
        w = jnp.concatenate([w_ref[2 * i], w_ref[2 * i + 1]], axis=1)
        v = chunk(V, i)
        acc_p[...] += nn_dot(p, v)
        acc_w[...] += nn_dot(w, v)

    def give(which, ty):
        def step(i, carry):
            tz = around(i)
            src = outsend.at[which, ty * Z + tz]
            dst = outland.at[which, z * J + y]
            here = jnp.logical_and(tz == z, y == ty)

            @pl.when(here)
            def _():
                pltpu.make_async_copy(src, dst, osem.at[which]).start()

            @pl.when(jnp.logical_not(here))
            def _():
                pltpu.make_async_remote_copy(
                    src_ref=src, dst_ref=dst, send_sem=osend.at[which], recv_sem=osem.at[which],
                    device_id=device(x, ty, tz, c),
                ).start()

            return carry

        lax.fori_loop(0, Z, step, 0)

    rotate(k_in, K, True)
    pl.semaphore_wait(barrier, Y * Z - 1 + 3)
    direct(0)
    rotate(kt_in, KT)

    @pl.when(computes)
    def _():
        remote = heads - 1

        def begin(g, a):
            wait_direct(g)
            start_own(a)
            sent(g, remote)

        def loop(work):
            def step(i, carry):
                work(i)
                return carry

            lax.fori_loop(0, chunks, step, 0)

        begin(0, K)
        direct(1)
        rotate(q_in, Q)
        rotate(qt_in, QT)
        events(K, 2, 4)
        place(v_in, V)
        place(vt_in, VT)
        events(K, 4, 6)
        begin(1, KT)
        direct(2)
        mx[...] = jnp.full_like(mx, LOW)
        lsum[...] = jnp.zeros_like(lsum)
        gsum[...] = jnp.zeros_like(gsum)
        acc_p[...] = jnp.zeros_like(acc_p)
        acc_w[...] = jnp.zeros_like(acc_w)
        acc_t[...] = jnp.zeros_like(acc_t)
        events(K, 6, 8)
        events(KT, 2, 6)
        wait_direct(2)
        sent(2, remote)
        direct(3)
        wait_sibs(K)

        def first(i):
            @pl.when(jnp.logical_or(i == 2, i == 3))
            def _():
                event(KT, i + 4)

            @pl.when(i == 6)
            def _():
                begin(3, V)
                direct(4)

            scores(i)

        loop(first)
        mx[...] = jnp.broadcast_to(jnp.max(mx[...], axis=1, keepdims=True) * scale2, mx.shape)
        wait_sibs(KT)

        def second(i):
            @pl.when(i < 6)
            def _():
                event(V, i + 2)

            @pl.when(i == 6)
            def _():
                begin(4, VT)

            weights(i)

        loop(second)
        wait_sibs(V)

        def third(i):
            @pl.when(jnp.logical_or(i == 2, i == 3))
            def _():
                event(VT, i)

            value_products(i)

        loop(third)
        inverse = 1.0 / jnp.sum(lsum[...], axis=1, keepdims=True)
        slope = jnp.sum(gsum[...], axis=1, keepdims=True) * inverse * scale
        attended = acc_p[...] * inverse
        outsend[0] = attended.astype(jnp.bfloat16).reshape(Y * Z, ROWS, HD)
        for ty in range(Y):
            give(0, ty)
        lsum[...] = jnp.broadcast_to(inverse, lsum.shape)
        acc_w[...] = acc_w[...] * (inverse * scale) - slope * attended

        def fourth(i):
            @pl.when(i >= 4)
            def _():
                event(VT, i)

            wait_sib(VT, i)
            sx, u = origin(i)
            mine = (sx * C + c) * 2 + u
            other = (sx * C + 1 - c) * 2 + u
            acc_t[...] += nn_dot(
                jnp.concatenate([p_ref[mine], p_ref[other]], axis=1),
                jnp.concatenate([unit(VT, mine), unit(VT, other)], axis=0),
            )

        loop(fourth)
        for ty in range(Y):
            rows = slice(ty * span, (ty + 1) * span)
            tangent = acc_t[rows] * lsum[rows] + acc_w[rows]
            outsend[1, ty * Z : (ty + 1) * Z] = tangent.astype(jnp.bfloat16).reshape(Z, ROWS, HD)
            give(1, ty)

    @pl.when(jnp.logical_not(computes))
    def _():
        sent(0, heads)
        direct(1)
        rotate(q_in, Q)
        rotate(qt_in, QT)
        sent(1, heads)
        direct(2)
        place(v_in, V)
        place(vt_in, VT)
        sent(2, heads)
        direct(3)
        sent(3, heads)
        direct(4)
        sent(4, heads)

    def finish(which, out):
        pltpu.make_async_copy(outland.at[which], outland.at[which], osem.at[which]).wait()
        for h in range(heads):
            final[which, :, h * HD : (h + 1) * HD] = outland[which, h]
        pltpu.make_async_copy(final.at[which], out, fsem.at[which]).start()

    finish(0, o_out)
    finish(1, ot_out)
    pltpu.make_async_copy(final.at[0], o_out, fsem.at[0]).wait()
    pltpu.make_async_copy(final.at[1], ot_out, fsem.at[1]).wait()

    @pl.when(computes)
    def _():
        for n in range(4):
            part = kv.at[0, pl.ds(0, 6 * half)]
            pltpu.make_async_copy(part, part, rsend.at[n]).wait()
            part = kv.at[0, pl.ds(0, 8 * half)]
            pltpu.make_async_copy(part, part, bsend.at[n]).wait()
        for which in range(2):
            part = outsend.at[which, pl.ds(0, Y * Z - 1)]
            pltpu.make_async_copy(part, part, osend.at[which]).wait()


def shards(queries, key_vectors, values, query_tangent, key_tangent, value_tangent,
           frame_index, valid_counts):
    Z = ZH * ZL
    heads = Z * J
    span = Z * ROWS
    rows = Y * span
    chunks = X * C
    hbm = pl.BlockSpec(memory_space=pl.ANY)
    smem = pl.BlockSpec(memory_space=pltpu.SMEM)
    out = jax.ShapeDtypeStruct((ROWS, heads * HD), jnp.bfloat16)
    return pl.pallas_call(
        kernel,
        out_shape=(out, out),
        in_specs=[hbm] * 6 + [smem] * 2,
        out_specs=(hbm, hbm),
        scratch_shapes=[
            pltpu.VMEM((6, ROWS, heads * HD), jnp.bfloat16),
            pltpu.VMEM((heads, 6, ROWS, HD), jnp.bfloat16),
            pltpu.VMEM((6, chunks * Y, span, HD), jnp.bfloat16),
            pltpu.VMEM((chunks, rows, rows), jnp.float32),
            pltpu.VMEM((2 * chunks, rows, rows // 2), jnp.bfloat16),
            pltpu.VMEM((2 * chunks, rows, rows // 2), jnp.bfloat16),
            pltpu.VMEM((rows, HD), jnp.float32),
            pltpu.VMEM((rows, HD), jnp.float32),
            pltpu.VMEM((rows, HD), jnp.float32),
            pltpu.VMEM((rows, HD), jnp.float32),
            pltpu.VMEM((rows, HD), jnp.float32),
            pltpu.VMEM((rows, HD), jnp.float32),
            pltpu.VMEM((2, Y * Z, ROWS, HD), jnp.bfloat16),
            pltpu.VMEM((2, heads, ROWS, HD), jnp.bfloat16),
            pltpu.VMEM((2, ROWS, heads * HD), jnp.bfloat16),
            pltpu.SemaphoreType.DMA((6,)),
            pltpu.SemaphoreType.DMA((5,)),
            pltpu.SemaphoreType.DMA((4, 8)),
            pltpu.SemaphoreType.DMA((4, 8)),
            pltpu.SemaphoreType.DMA((5,)),
            pltpu.SemaphoreType.DMA((4,)),
            pltpu.SemaphoreType.DMA((4,)),
            pltpu.SemaphoreType.DMA((2,)),
            pltpu.SemaphoreType.DMA((2,)),
            pltpu.SemaphoreType.DMA((2,)),
        ],
        compiler_params=pltpu.CompilerParams(
            collective_id=0, has_side_effects=True, vmem_limit_bytes=52 * 1024 * 1024
        ),
    )(queries, key_vectors, values, query_tangent, key_tangent, value_tangent,
      frame_index, valid_counts)


def solution(mesh):
    tokens = P(("blk", "head"), None)
    return jax.shard_map(
        shards,
        mesh=mesh,
        in_specs=(tokens,) * 6 + (P("blk"), P("blk")),
        out_specs=(tokens, tokens),
        check_vma=False,
    )
```

```python
import math

import jax
import jax.numpy as jnp
from jax import lax
from jax.experimental import pallas as pl
from jax.experimental.pallas import tpu as pltpu
from jax.sharding import PartitionSpec as P

HD = 128
FRAME_TOKENS = 3600
GRID_WIDTH = 80
ROWS = 16

X, Y, ZH, ZL, C = 4, 4, 2, 4, 2
J = 3

MARK = 16384.0
MARK_SUM = 1.0e5
LOW = -1.0e30

K, KT, Q, QT, V, VT = range(6)
GROUPS = ((K, 1), (KT, 1), (V, 1), (Q, 2), (VT, 1))
GROUP_OF = {K: 0, KT: 1, V: 2, Q: 3, VT: 4}
RING = (K, KT, V, VT)


def device(x, y, z, c):
    return (y * (ZH * X) + lax.div(z, ZL) * X + x, lax.rem(z, ZL) * C + c)


def nt_dot(a, b):
    return lax.dot_general(a, b, (((1,), (1,)), ((), ())), preferred_element_type=jnp.float32)


def nn_dot(a, b):
    return jnp.dot(a, b, preferred_element_type=jnp.float32)


def kernel(
    q_in, k_in, v_in, qt_in, kt_in, vt_in, frame_ref, count_ref,
    o_out, ot_out,
    raw, send, kv, s_ref, p_ref, w_ref, acc_p, acc_w, acc_t, mx, lsum, gsum, outsend, outland, final,
    isem, dsem, rsem, ssem, dsend, rsend, bsend, osem, osend, fsem,
):
    Z = ZH * ZL
    heads = Z * J
    span = Z * ROWS
    chunks = X * C
    near = Z // 2
    rows = Y * span
    side = rows // 2
    scale = 1.0 / math.sqrt(HD)
    scale2 = scale * math.log2(math.e)

    blk = lax.axis_index("blk")
    hd = lax.axis_index("head")
    x = lax.rem(blk, X)
    y = lax.div(blk, ZH * X)
    z = lax.rem(lax.div(blk, X), ZH) * ZL + lax.div(hd, C)
    c = lax.rem(hd, C)
    right = device(lax.rem(x + 1, X), y, z, c)
    left = device(lax.rem(x + X - 1, X), y, z, c)
    sib = device(x, y, z, 1 - c)
    own = (x * C + c) * 2
    computes = y < J

    def fetch(ref, slot):
        return pltpu.make_async_copy(ref, raw.at[slot], isem.at[slot])

    inputs = ((k_in, K), (kt_in, KT), (v_in, V), (q_in, Q), (qt_in, QT), (vt_in, VT))
    for ref, slot in inputs:
        fetch(ref, slot).start()

    barrier = pltpu.get_barrier_semaphore()

    def greet(i, carry):
        gz = lax.rem(z + near + i, Z)
        for gy in range(Y):

            @pl.when(jnp.logical_or(gy != y, gz != z))
            def _():
                pl.semaphore_signal(barrier, inc=1, device_id=device(x, gy, gz, c))

        return carry

    lax.fori_loop(0, Z, greet, 0)
    for other in (right, left, sib):
        pl.semaphore_signal(barrier, inc=1, device_id=other)

    row = lax.broadcasted_iota(jnp.int32, (ROWS, HD), 0)
    lane = lax.broadcasted_iota(jnp.int32, (ROWS, HD), 1)
    frame = jnp.zeros((ROWS, HD), jnp.float32)
    for i in range(ROWS):
        frame = jnp.where(row == i, frame_ref[hd * ROWS + i].astype(jnp.float32), frame)
    valid = hd * ROWS + row < count_ref[0]
    token = blk * (ROWS * ZL * C) + hd * ROWS + row
    token = jnp.where(token >= FRAME_TOKENS, token - FRAME_TOKENS, token).astype(jnp.float32)
    height = jnp.floor((token + 0.5) * (1.0 / GRID_WIDTH))
    across = token - height * GRID_WIDTH
    pair = lax.rem(lane, HD // 2)
    spatial = HD // 6
    temporal = HD // 2 - 2 * spatial
    is_frame = pair < temporal
    is_height = pair < temporal + spatial
    index = jnp.where(is_frame, pair, jnp.where(is_height, pair - temporal, pair - temporal - spatial))
    count = jnp.where(is_frame, float(temporal), float(spatial))
    freqs = jnp.exp(-math.log(10000.0) * index.astype(jnp.float32) / count)
    angles = jnp.where(is_frame, frame, jnp.where(is_height, height, across)) * freqs
    cosine = jnp.cos(angles)
    sine = jnp.sin(angles)
    sine = jnp.where(lane < HD // 2, -sine, sine)

    def rotate(ref, slot, marked=False):
        fetch(ref, slot).wait()
        for h in range(heads):
            wide = raw[slot, :, h * HD : (h + 1) * HD].astype(jnp.float32)
            turned = wide * cosine + pltpu.roll(wide, HD // 2, 1) * sine
            if marked:
                turned = jnp.where(valid, turned, MARK)
            send[h, slot] = turned.astype(jnp.bfloat16)

    def place(ref, slot):
        fetch(ref, slot).wait()
        for h in range(heads):
            send[h, slot] = raw[slot, :, h * HD : (h + 1) * HD]

    def direct(a):
        g = GROUP_OF[a]
        first, count = GROUPS[g]

        def step(i, carry):
            tz = lax.rem(z + 2 + Z - i, Z)
            u = lax.div(i, near)
            slot = lax.rem(i, near)
            for j in range(J):
                src = send.at[tz * J + j, pl.ds(first, count)]
                dst = kv.at[pl.ds(first, count), own + u, y, pl.ds(slot * ROWS, ROWS)]
                here = jnp.logical_and(tz == z, y == j)

                @pl.when(here)
                def _():
                    pltpu.make_async_copy(src, dst, dsem.at[g, u]).start()

                @pl.when(jnp.logical_not(here))
                def _():
                    pltpu.make_async_remote_copy(
                        src_ref=src, dst_ref=dst, send_sem=dsend.at[g], recv_sem=dsem.at[g, u],
                        device_id=device(x, j, tz, c),
                    ).start()

            return carry

        lax.fori_loop(0, Z, step, 0)

    def wait_direct(a, u):
        g = GROUP_OF[a]
        first, count = GROUPS[g]
        region = kv.at[pl.ds(first, count), own + u]
        pltpu.make_async_copy(region, region, dsem.at[g, u]).wait()

    def ring_send(a, part, to, event):
        n = RING.index(a)
        pltpu.make_async_remote_copy(
            src_ref=part, dst_ref=part, send_sem=rsend.at[n], recv_sem=rsem.at[n, event],
            device_id=to,
        ).start()

    def sib_send(a, part, event):
        n = RING.index(a)
        pltpu.make_async_remote_copy(
            src_ref=part, dst_ref=part, send_sem=bsend.at[n], recv_sem=ssem.at[n, event],
            device_id=sib,
        ).start()

    def origin(i):
        far = jnp.where(i >= 6, 2, jnp.where(i >= 2, 1, 0))
        even = lax.rem(i, 2) == 0
        sx = lax.rem(jnp.where(even, x + X - far, x + far), X)
        swap = jnp.logical_or(i == 4, i == 5)
        u = jnp.where(jnp.logical_xor(even, swap), 0, 1)
        return sx, u

    def places(i):
        sx, u = origin(i)
        return (sx * C + c) * 2 + u, (sx * C + 1 - c) * 2 + u

    def start(a, u):
        wait_direct(a, u)
        part = kv.at[a, own + u]
        if u == 0:
            ring_send(a, part, right, 2)
            ring_send(a, part, left, 5)
        else:
            ring_send(a, part, left, 3)
            ring_send(a, part, right, 4)
        sib_send(a, part, u)

    def take(a, i):
        part = kv.at[a, places(jnp.int32(i))[0]]
        pltpu.make_async_copy(part, part, rsem.at[RING.index(a), i]).wait()
        if i == 2:
            ring_send(a, part, right, 6)
        if i == 3:
            ring_send(a, part, left, 7)
        sib_send(a, part, i)

    def wait_sib(a, i):
        part = kv.at[a, places(i)[1]]
        pltpu.make_async_copy(part, part, ssem.at[RING.index(a), i]).wait()

    def queries_of(a):
        return kv[a, pl.ds(own, 2)].reshape(rows, HD)

    def pair(a, i):
        mine, other = places(i)
        return jnp.concatenate(
            [kv[a, mine].reshape(side, HD), kv[a, other].reshape(side, HD)], axis=0
        )

    def lanes(op, total, array):
        for t in range(array.shape[1] // HD):
            total = op(total, array[:, t * HD : (t + 1) * HD])
        return total

    def scores(i):
        keys = pair(K, i)
        s = nt_dot(queries_of(Q), keys)
        parts = []
        for n in range(2):
            low, high = n * side, (n + 1) * side
            marks = nt_dot(jnp.ones((8, HD), jnp.bfloat16), keys[high - HD : high])[0:1]
            parts.append(s[:, low : high - HD])
            parts.append(jnp.where(marks > MARK_SUM, LOW, s[:, high - HD : high]))
        s = jnp.concatenate(parts, axis=1)
        s_ref[i] = s
        mx[...] = lanes(jnp.maximum, mx[...], s)

    def weights(i):
        top = jnp.concatenate([mx[...]] * (rows // HD), axis=1)
        p = jnp.exp2(s_ref[i] * scale2 - top)
        g = nt_dot(
            jnp.concatenate([queries_of(QT), queries_of(Q)], axis=1),
            jnp.concatenate([pair(K, i), pair(KT, i)], axis=1),
        )
        w = p * g
        lsum[...] = lanes(jnp.add, lsum[...], p)
        gsum[...] = lanes(jnp.add, gsum[...], w)
        p_ref[i] = p.astype(jnp.bfloat16)
        w_ref[i] = w.astype(jnp.bfloat16)

    def value_products(i):
        v = pair(V, i)
        acc_p[...] += nn_dot(p_ref[i], v)
        acc_w[...] += nn_dot(w_ref[i], v)

    def give(which, u):
        def step(k, carry):
            tz = lax.rem(z + u * near + k + Z - 2, Z)
            for ty in range(Y):
                src = outsend.at[which, (u * Y + ty) * near + k]
                dst = outland.at[which, z * J + y]
                here = jnp.logical_and(tz == z, y == ty)

                @pl.when(here)
                def _():
                    pltpu.make_async_copy(src, dst, osem.at[which]).start()

                @pl.when(jnp.logical_not(here))
                def _():
                    pltpu.make_async_remote_copy(
                        src_ref=src, dst_ref=dst, send_sem=osend.at[which],
                        recv_sem=osem.at[which], device_id=device(x, ty, tz, c),
                    ).start()

            return carry

        lax.fori_loop(0, near, step, 0)

    def loop(work, beside):
        def step(i, carry):
            for k, act in beside.items():
                pl.when(i == k)(act)
            work(i)
            return carry

        lax.fori_loop(0, chunks, step, 0)

    rotate(k_in, K, True)
    pl.semaphore_wait(barrier, Y * Z - 1 + 3)
    direct(K)
    rotate(kt_in, KT)
    direct(KT)
    place(v_in, V)
    direct(V)

    @pl.when(computes)
    def _():
        start(K, 0)
        rotate(q_in, Q)
        rotate(qt_in, QT)
        direct(Q)
        start(K, 1)
        place(vt_in, VT)
        direct(VT)
        start(KT, 0)
        mx[...] = jnp.full_like(mx, LOW)
        for ref in (lsum, gsum, acc_p, acc_w, acc_t):
            ref[...] = jnp.zeros_like(ref)
        take(K, 2)
        take(K, 3)
        start(KT, 1)
        take(K, 4)
        take(K, 5)
        start(V, 0)
        take(KT, 2)
        take(KT, 3)
        start(V, 1)
        take(K, 6)
        take(K, 7)
        take(KT, 4)
        take(KT, 5)
        wait_direct(Q, 0)
        wait_direct(Q, 1)

        def first(i):
            wait_sib(K, i)
            scores(i)

        loop(first, {
            1: lambda: start(VT, 0),
            2: lambda: take(V, 2),
            3: lambda: take(V, 3),
            4: lambda: start(VT, 1),
            5: lambda: take(KT, 6),
            6: lambda: take(KT, 7),
        })
        mx[...] = jnp.broadcast_to(jnp.max(mx[...], axis=1, keepdims=True) * scale2, mx.shape)

        def second(i):
            wait_sib(KT, i)
            weights(i)

        loop(second, {
            0: lambda: take(V, 4),
            1: lambda: take(V, 5),
            3: lambda: take(VT, 2),
            4: lambda: take(VT, 3),
            5: lambda: take(V, 6),
            6: lambda: take(V, 7),
        })

        def third(i):
            wait_sib(V, i)
            value_products(i)

        loop(third, {3: lambda: take(VT, 4), 4: lambda: take(VT, 5)})
        inverse = 1.0 / jnp.sum(lsum[...], axis=1, keepdims=True)
        slope = jnp.sum(gsum[...], axis=1, keepdims=True) * inverse * scale
        attended = acc_p[...] * inverse
        outsend[0] = attended.astype(jnp.bfloat16).reshape(Y * Z, ROWS, HD)
        give(0, 1)
        give(0, 0)
        lsum[...] = jnp.broadcast_to(inverse, lsum.shape)
        acc_w[...] = acc_w[...] * (inverse * scale) - slope * attended

        def fourth(i):
            wait_sib(VT, i)
            acc_t[...] += nn_dot(p_ref[i], pair(VT, i))

        loop(fourth, {6: lambda: take(VT, 6), 7: lambda: take(VT, 7)})
        for u in (1, 0):
            part = slice(u * side, (u + 1) * side)
            tangent = acc_t[part] * lsum[part] + acc_w[part]
            outsend[1, u * Y * near : (u + 1) * Y * near] = tangent.astype(
                jnp.bfloat16
            ).reshape(Y * near, ROWS, HD)
            give(1, u)

    @pl.when(jnp.logical_not(computes))
    def _():
        rotate(q_in, Q)
        rotate(qt_in, QT)
        direct(Q)
        place(vt_in, VT)
        direct(VT)

    def finish(which, out):
        pltpu.make_async_copy(outland.at[which], outland.at[which], osem.at[which]).wait()
        for h in range(heads):
            final[which, :, h * HD : (h + 1) * HD] = outland[which, h]
        pltpu.make_async_copy(final.at[which], out, fsem.at[which]).start()

    finish(0, o_out)
    finish(1, ot_out)

    def sent(count):
        for g, (first, arrays) in enumerate(GROUPS):
            part = send.at[pl.ds(0, count), pl.ds(first, arrays)]
            pltpu.make_async_copy(part, part, dsend.at[g]).wait()

    @pl.when(computes)
    def _():
        sent(heads - 1)
        for n in range(4):
            part = kv.at[0, pl.ds(0, 6)]
            pltpu.make_async_copy(part, part, rsend.at[n]).wait()
            part = kv.at[0, pl.ds(0, 8)]
            pltpu.make_async_copy(part, part, bsend.at[n]).wait()
        for which in range(2):
            part = outsend.at[which, pl.ds(0, Y * Z - 1)]
            pltpu.make_async_copy(part, part, osend.at[which]).wait()

    @pl.when(jnp.logical_not(computes))
    def _():
        sent(heads)

    pltpu.make_async_copy(final.at[0], o_out, fsem.at[0]).wait()
    pltpu.make_async_copy(final.at[1], ot_out, fsem.at[1]).wait()


def shards(queries, key_vectors, values, query_tangent, key_tangent, value_tangent,
           frame_index, valid_counts):
    Z = ZH * ZL
    heads = Z * J
    span = Z * ROWS
    rows = Y * span
    chunks = X * C
    hbm = pl.BlockSpec(memory_space=pl.ANY)
    smem = pl.BlockSpec(memory_space=pltpu.SMEM)
    out = jax.ShapeDtypeStruct((ROWS, heads * HD), jnp.bfloat16)
    return pl.pallas_call(
        kernel,
        out_shape=(out, out),
        in_specs=[hbm] * 6 + [smem] * 2,
        out_specs=(hbm, hbm),
        scratch_shapes=[
            pltpu.VMEM((6, ROWS, heads * HD), jnp.bfloat16),
            pltpu.VMEM((heads, 6, ROWS, HD), jnp.bfloat16),
            pltpu.VMEM((6, chunks * 2, Y, span // 2, HD), jnp.bfloat16),
            pltpu.VMEM((chunks, rows, rows), jnp.float32),
            pltpu.VMEM((chunks, rows, rows), jnp.bfloat16),
            pltpu.VMEM((chunks, rows, rows), jnp.bfloat16),
            pltpu.VMEM((rows, HD), jnp.float32),
            pltpu.VMEM((rows, HD), jnp.float32),
            pltpu.VMEM((rows, HD), jnp.float32),
            pltpu.VMEM((rows, HD), jnp.float32),
            pltpu.VMEM((rows, HD), jnp.float32),
            pltpu.VMEM((rows, HD), jnp.float32),
            pltpu.VMEM((2, Y * Z, ROWS, HD), jnp.bfloat16),
            pltpu.VMEM((2, heads, ROWS, HD), jnp.bfloat16),
            pltpu.VMEM((2, ROWS, heads * HD), jnp.bfloat16),
            pltpu.SemaphoreType.DMA((6,)),
            pltpu.SemaphoreType.DMA((5, 2)),
            pltpu.SemaphoreType.DMA((4, 8)),
            pltpu.SemaphoreType.DMA((4, 8)),
            pltpu.SemaphoreType.DMA((5,)),
            pltpu.SemaphoreType.DMA((4,)),
            pltpu.SemaphoreType.DMA((4,)),
            pltpu.SemaphoreType.DMA((2,)),
            pltpu.SemaphoreType.DMA((2,)),
            pltpu.SemaphoreType.DMA((2,)),
        ],
        compiler_params=pltpu.CompilerParams(
            collective_id=0, has_side_effects=True, vmem_limit_bytes=64 * 1024 * 1024
        ),
    )(queries, key_vectors, values, query_tangent, key_tangent, value_tangent,
      frame_index, valid_counts)


def solution(mesh):
    tokens = P(("blk", "head"), None)
    return jax.shard_map(
        shards,
        mesh=mesh,
        in_specs=(tokens,) * 6 + (P("blk"), P("blk")),
        out_specs=(tokens, tokens),
        check_vma=False,
    )
```

```python
import math

import jax
import jax.numpy as jnp
from jax import lax
from jax.experimental import pallas as pl
from jax.experimental.pallas import tpu as pltpu
from jax.sharding import PartitionSpec as P

HD = 128
FRAME_TOKENS = 3600
GRID_WIDTH = 80
ROWS = 16

X, Y, ZH, ZL, C = 4, 4, 2, 4, 2
J = 3

MARK = 16384.0
MARK_FLOOR = 1000.0
MARK_WEIGHT = -1048576.0
LOW = -1.0e30

K, KT, Q, QT, V, VT = range(6)
GROUPS = ((K, 1), (KT, 1), (V, 1), (Q, 2), (VT, 1))
GROUP_OF = {K: 0, KT: 1, V: 2, Q: 3, VT: 4}
RING = (K, KT, V, VT)


def device(x, y, z, c):
    return (y * (ZH * X) + lax.div(z, ZL) * X + x, lax.rem(z, ZL) * C + c)


def nt_dot(a, b):
    return lax.dot_general(a, b, (((1,), (1,)), ((), ())), preferred_element_type=jnp.float32)


def nn_dot(a, b):
    return jnp.dot(a, b, preferred_element_type=jnp.float32)


def kernel(
    q_in, k_in, v_in, qt_in, kt_in, vt_in, frame_ref, count_ref,
    o_out, ot_out,
    raw, send, kv, s_ref, p_ref, w_ref, acc_p, acc_w, acc_t, mx, lsum, gsum, outsend, outland, final,
    isem, dsem, rsem, ssem, dsend, rsend, bsend, osem, osend, fsem,
):
    Z = ZH * ZL
    heads = Z * J
    span = Z * ROWS
    chunks = X * C
    near = Z // 2
    rows = Y * span
    side = rows // 2
    scale = 1.0 / math.sqrt(HD)
    scale2 = scale * math.log2(math.e)

    blk = lax.axis_index("blk")
    hd = lax.axis_index("head")
    x = lax.rem(blk, X)
    y = lax.div(blk, ZH * X)
    z = lax.rem(lax.div(blk, X), ZH) * ZL + lax.div(hd, C)
    c = lax.rem(hd, C)
    right = device(lax.rem(x + 1, X), y, z, c)
    left = device(lax.rem(x + X - 1, X), y, z, c)
    sib = device(x, y, z, 1 - c)
    own = (x * C + c) * 2
    computes = y < J

    def fetch(ref, slot):
        return pltpu.make_async_copy(ref, raw.at[slot], isem.at[slot])

    inputs = ((k_in, K), (kt_in, KT), (v_in, V), (q_in, Q), (qt_in, QT), (vt_in, VT))
    for ref, slot in inputs:
        fetch(ref, slot).start()

    barrier = pltpu.get_barrier_semaphore()

    def greet(i, carry):
        gz = lax.rem(z + near + i, Z)
        for gy in range(Y):

            @pl.when(jnp.logical_or(gy != y, gz != z))
            def _():
                pl.semaphore_signal(barrier, inc=1, device_id=device(x, gy, gz, c))

        return carry

    lax.fori_loop(0, Z, greet, 0)
    for other in (right, left, sib):
        pl.semaphore_signal(barrier, inc=1, device_id=other)

    row = lax.broadcasted_iota(jnp.int32, (ROWS, HD), 0)
    lane = lax.broadcasted_iota(jnp.int32, (ROWS, HD), 1)
    frame = jnp.zeros((ROWS, HD), jnp.float32)
    for i in range(ROWS):
        frame = jnp.where(row == i, frame_ref[hd * ROWS + i].astype(jnp.float32), frame)
    valid = hd * ROWS + row < count_ref[0]
    token = blk * (ROWS * ZL * C) + hd * ROWS + row
    token = jnp.where(token >= FRAME_TOKENS, token - FRAME_TOKENS, token).astype(jnp.float32)
    height = jnp.floor((token + 0.5) * (1.0 / GRID_WIDTH))
    across = token - height * GRID_WIDTH
    pair = lax.rem(lane, HD // 2)
    spatial = HD // 6
    temporal = HD // 2 - 2 * spatial
    is_frame = pair < temporal
    is_height = pair < temporal + spatial
    index = jnp.where(is_frame, pair, jnp.where(is_height, pair - temporal, pair - temporal - spatial))
    count = jnp.where(is_frame, float(temporal), float(spatial))
    freqs = jnp.exp(-math.log(10000.0) * index.astype(jnp.float32) / count)
    angles = jnp.where(is_frame, frame, jnp.where(is_height, height, across)) * freqs
    cosine = jnp.cos(angles)
    sine = jnp.sin(angles)
    sine = jnp.where(lane < HD // 2, -sine, sine)

    def rotate(ref, slot, marked=False):
        fetch(ref, slot).wait()
        for h in range(heads):
            wide = raw[slot, :, h * HD : (h + 1) * HD].astype(jnp.float32)
            turned = wide * cosine + pltpu.roll(wide, HD // 2, 1) * sine
            if marked:
                turned = jnp.where(valid, turned, MARK)
            send[h, slot] = turned.astype(jnp.bfloat16)

    def place(ref, slot):
        fetch(ref, slot).wait()
        for h in range(heads):
            send[h, slot] = raw[slot, :, h * HD : (h + 1) * HD]

    def direct(a):
        g = GROUP_OF[a]
        first, count = GROUPS[g]

        def step(i, carry):
            tz = lax.rem(z + 2 + Z - i, Z)
            u = lax.div(i, near)
            slot = lax.rem(i, near)
            for j in range(J):
                src = send.at[tz * J + j, pl.ds(first, count)]
                dst = kv.at[pl.ds(first, count), own + u, y, pl.ds(slot * ROWS, ROWS)]
                here = jnp.logical_and(tz == z, y == j)

                @pl.when(here)
                def _():
                    pltpu.make_async_copy(src, dst, dsem.at[g, u]).start()

                @pl.when(jnp.logical_not(here))
                def _():
                    pltpu.make_async_remote_copy(
                        src_ref=src, dst_ref=dst, send_sem=dsend.at[g], recv_sem=dsem.at[g, u],
                        device_id=device(x, j, tz, c),
                    ).start()

            return carry

        lax.fori_loop(0, Z, step, 0)

    def wait_direct(a, u):
        g = GROUP_OF[a]
        first, count = GROUPS[g]
        region = kv.at[pl.ds(first, count), own + u]
        pltpu.make_async_copy(region, region, dsem.at[g, u]).wait()

    def ring_send(a, part, to, event):
        n = RING.index(a)
        pltpu.make_async_remote_copy(
            src_ref=part, dst_ref=part, send_sem=rsend.at[n], recv_sem=rsem.at[n, event],
            device_id=to,
        ).start()

    def sib_send(a, part, event):
        n = RING.index(a)
        pltpu.make_async_remote_copy(
            src_ref=part, dst_ref=part, send_sem=bsend.at[n], recv_sem=ssem.at[n, event],
            device_id=sib,
        ).start()

    def origin(i):
        step = jnp.where(lax.rem(i, 2) == 0, X - 1, 1)
        sx = lax.rem(x + jnp.where(i < 2, 0, jnp.where(i < 6, step, 2)), X)
        u = jnp.where(i < 2, i, jnp.where(i < 6, lax.div(i - 2, 2), i - 6))
        return sx, u

    def places(i):
        sx, u = origin(i)
        return (sx * C + c) * 2 + u, (sx * C + 1 - c) * 2 + u

    def start(a, u):
        wait_direct(a, u)
        part = kv.at[a, own + u]
        ring_send(a, part, right, 2 + 2 * u)
        ring_send(a, part, left, 3 + 2 * u)
        sib_send(a, part, u)

    def take(a, i):
        n = RING.index(a)
        place = places(jnp.int32(i))[0]
        part = kv.at[a, place]
        halves = kv.at[a, place, pl.ds(0, Y // 2)], kv.at[a, place, pl.ds(Y // 2, Y // 2)]
        if i < 6:
            pltpu.make_async_copy(part, part, rsem.at[n, i]).wait()
            u = (i - 2) // 2
            if i % 2 == 0:
                ring_send(a, halves[0], right, 6 + 2 * u)
            else:
                ring_send(a, halves[1], left, 7 + 2 * u)
        else:
            u = i - 6
            for side_of, half in enumerate(halves):
                pltpu.make_async_copy(half, half, rsem.at[n, 6 + 2 * u + side_of]).wait()
        sib_send(a, part, i)

    def wait_sib(a, i):
        part = kv.at[a, places(i)[1]]
        pltpu.make_async_copy(part, part, ssem.at[RING.index(a), i]).wait()

    def queries_of(a):
        return kv[a, pl.ds(own, 2)].reshape(rows, HD)

    def units(a, j):
        parts = []
        for n in range(2):
            for place in places(2 * j + n):
                parts.append(kv[a, place].reshape(side, HD))
        return parts

    def wait_sibs(a, j):
        wait_sib(a, 2 * j)
        wait_sib(a, 2 * j + 1)

    def lanes(op, total, array):
        for t in range(array.shape[1] // HD):
            total = op(total, array[:, t * HD : (t + 1) * HD])
        return total

    def scores(j):
        wait_sibs(K, j)
        keys = units(K, j)
        last = side // Y
        marks = []
        for part in keys:
            over = jnp.maximum(part[side - last :].astype(jnp.float32) - MARK_FLOOR, 0.0)
            marks.append(jnp.zeros((side - last, HD), jnp.bfloat16))
            marks.append(over.astype(jnp.bfloat16))
        weight = jnp.full((rows, HD), MARK_WEIGHT, jnp.bfloat16)
        s = nt_dot(
            jnp.concatenate([queries_of(Q), weight], axis=1),
            jnp.concatenate([jnp.concatenate(keys, axis=0), jnp.concatenate(marks, axis=0)], axis=1),
        )
        s_ref[j] = s
        mx[...] = lanes(jnp.maximum, mx[...], s)

    def weights(j):
        wait_sibs(KT, j)
        top = jnp.concatenate([mx[...]] * (2 * rows // HD), axis=1)
        p = jnp.exp2(s_ref[j] * scale2 - top)
        g = nt_dot(
            jnp.concatenate([queries_of(QT), queries_of(Q)], axis=1),
            jnp.concatenate(
                [jnp.concatenate(units(K, j), axis=0), jnp.concatenate(units(KT, j), axis=0)], axis=1
            ),
        )
        w = p * g
        lsum[...] = lanes(jnp.add, lsum[...], p)
        gsum[...] = lanes(jnp.add, gsum[...], w)
        p_ref[j] = p.astype(jnp.bfloat16)
        w_ref[j] = w.astype(jnp.bfloat16)

    def stacked(a, steps):
        parts = []
        for j in steps:
            wait_sibs(a, j)
        for j in steps:
            parts += units(a, j)
        return jnp.concatenate(parts, axis=0)

    def product(ref, steps, right_side):
        return nn_dot(jnp.concatenate([ref[j] for j in steps], axis=1), right_side)

    def give(which, u):
        def step(k, carry):
            tz = lax.rem(z + u * near + k + Z - 2, Z)
            for ty in range(Y):
                src = outsend.at[which, (u * Y + ty) * near + k]
                dst = outland.at[which, z * J + y]
                here = jnp.logical_and(tz == z, y == ty)

                @pl.when(here)
                def _():
                    pltpu.make_async_copy(src, dst, osem.at[which]).start()

                @pl.when(jnp.logical_not(here))
                def _():
                    pltpu.make_async_remote_copy(
                        src_ref=src, dst_ref=dst, send_sem=osend.at[which],
                        recv_sem=osem.at[which], device_id=device(x, ty, tz, c),
                    ).start()

            return carry

        lax.fori_loop(0, near, step, 0)

    def loop(work, low, high, beside=None):
        def step(i, carry):
            for k, act in (beside or {}).items():
                pl.when(i == k)(act)
            work(i)
            return carry

        lax.fori_loop(low, high, step, 0)

    def both(a, i):
        take(a, i)
        take(a, i + 1)

    rotate(k_in, K, True)
    pl.semaphore_wait(barrier, Y * Z - 1 + 3)
    direct(K)
    rotate(kt_in, KT)
    direct(KT)
    place(v_in, V)
    direct(V)

    @pl.when(computes)
    def _():
        start(K, 0)
        rotate(q_in, Q)
        rotate(qt_in, QT)
        direct(Q)
        place(vt_in, VT)
        direct(VT)
        start(K, 1)
        start(KT, 0)
        start(KT, 1)
        mx[...] = jnp.full_like(mx, LOW)
        lsum[...] = jnp.zeros_like(lsum)
        gsum[...] = jnp.zeros_like(gsum)
        both(K, 2)
        start(V, 0)
        both(K, 4)
        start(V, 1)
        both(KT, 2)
        take(K, 6)
        both(KT, 4)
        wait_direct(Q, 0)
        wait_direct(Q, 1)

        def before_last():
            take(K, 7)
            both(V, 2)

        loop(scores, 0, 4, {
            1: lambda: start(VT, 0),
            2: lambda: start(VT, 1),
            3: before_last,
        })
        mx[...] = jnp.broadcast_to(jnp.max(mx[...], axis=1, keepdims=True) * scale2, mx.shape)
        loop(weights, 0, 4, {
            1: lambda: take(KT, 6),
            2: lambda: both(V, 4),
            3: lambda: take(KT, 7),
        })
        both(VT, 2)
        early, late = range(3), range(3, 4)
        v = stacked(V, early)
        acc_p[...] = product(p_ref, early, v)
        acc_w[...] = product(w_ref, early, v)
        both(VT, 4)
        both(V, 6)
        v = stacked(V, late)
        acc_p[...] += product(p_ref, late, v)
        acc_w[...] += product(w_ref, late, v)
        inverse = 1.0 / jnp.sum(lsum[...], axis=1, keepdims=True)
        slope = jnp.sum(gsum[...], axis=1, keepdims=True) * inverse * scale
        attended = acc_p[...] * inverse
        outsend[0] = attended.astype(jnp.bfloat16).reshape(Y * Z, ROWS, HD)
        give(0, 1)
        give(0, 0)
        lsum[...] = jnp.broadcast_to(inverse, lsum.shape)
        acc_w[...] = acc_w[...] * (inverse * scale) - slope * attended

        acc_t[...] = product(p_ref, early, stacked(VT, early))
        both(VT, 6)
        acc_t[...] += product(p_ref, late, stacked(VT, late))
        for u in (1, 0):
            part = slice(u * side, (u + 1) * side)
            tangent = acc_t[part] * lsum[part] + acc_w[part]
            outsend[1, u * Y * near : (u + 1) * Y * near] = tangent.astype(
                jnp.bfloat16
            ).reshape(Y * near, ROWS, HD)
            give(1, u)

    @pl.when(jnp.logical_not(computes))
    def _():
        rotate(q_in, Q)
        rotate(qt_in, QT)
        direct(Q)
        place(vt_in, VT)
        direct(VT)

    def finish(which, out):
        pltpu.make_async_copy(outland.at[which], outland.at[which], osem.at[which]).wait()
        for h in range(heads):
            final[which, :, h * HD : (h + 1) * HD] = outland[which, h]
        pltpu.make_async_copy(final.at[which], out, fsem.at[which]).start()

    finish(0, o_out)
    finish(1, ot_out)

    def sent(count):
        for g, (first, arrays) in enumerate(GROUPS):
            part = send.at[pl.ds(0, count), pl.ds(first, arrays)]
            pltpu.make_async_copy(part, part, dsend.at[g]).wait()

    @pl.when(computes)
    def _():
        sent(heads - 1)
        for n in range(4):
            part = kv.at[0, pl.ds(0, 6)]
            pltpu.make_async_copy(part, part, rsend.at[n]).wait()
            part = kv.at[0, pl.ds(0, 8)]
            pltpu.make_async_copy(part, part, bsend.at[n]).wait()
        for which in range(2):
            part = outsend.at[which, pl.ds(0, Y * Z - 1)]
            pltpu.make_async_copy(part, part, osend.at[which]).wait()

    @pl.when(jnp.logical_not(computes))
    def _():
        sent(heads)

    pltpu.make_async_copy(final.at[0], o_out, fsem.at[0]).wait()
    pltpu.make_async_copy(final.at[1], ot_out, fsem.at[1]).wait()


def shards(queries, key_vectors, values, query_tangent, key_tangent, value_tangent,
           frame_index, valid_counts):
    Z = ZH * ZL
    heads = Z * J
    span = Z * ROWS
    rows = Y * span
    chunks = X * C
    hbm = pl.BlockSpec(memory_space=pl.ANY)
    smem = pl.BlockSpec(memory_space=pltpu.SMEM)
    out = jax.ShapeDtypeStruct((ROWS, heads * HD), jnp.bfloat16)
    return pl.pallas_call(
        kernel,
        out_shape=(out, out),
        in_specs=[hbm] * 6 + [smem] * 2,
        out_specs=(hbm, hbm),
        scratch_shapes=[
            pltpu.VMEM((6, ROWS, heads * HD), jnp.bfloat16),
            pltpu.VMEM((heads, 6, ROWS, HD), jnp.bfloat16),
            pltpu.VMEM((6, chunks * 2, Y, span // 2, HD), jnp.bfloat16),
            pltpu.VMEM((chunks // 2, rows, 2 * rows), jnp.float32),
            pltpu.VMEM((chunks // 2, rows, 2 * rows), jnp.bfloat16),
            pltpu.VMEM((chunks // 2, rows, 2 * rows), jnp.bfloat16),
            pltpu.VMEM((rows, HD), jnp.float32),
            pltpu.VMEM((rows, HD), jnp.float32),
            pltpu.VMEM((rows, HD), jnp.float32),
            pltpu.VMEM((rows, HD), jnp.float32),
            pltpu.VMEM((rows, HD), jnp.float32),
            pltpu.VMEM((rows, HD), jnp.float32),
            pltpu.VMEM((2, Y * Z, ROWS, HD), jnp.bfloat16),
            pltpu.VMEM((2, heads, ROWS, HD), jnp.bfloat16),
            pltpu.VMEM((2, ROWS, heads * HD), jnp.bfloat16),
            pltpu.SemaphoreType.DMA((6,)),
            pltpu.SemaphoreType.DMA((5, 2)),
            pltpu.SemaphoreType.DMA((4, 10)),
            pltpu.SemaphoreType.DMA((4, 8)),
            pltpu.SemaphoreType.DMA((5,)),
            pltpu.SemaphoreType.DMA((4,)),
            pltpu.SemaphoreType.DMA((4,)),
            pltpu.SemaphoreType.DMA((2,)),
            pltpu.SemaphoreType.DMA((2,)),
            pltpu.SemaphoreType.DMA((2,)),
        ],
        compiler_params=pltpu.CompilerParams(
            collective_id=0, has_side_effects=True, vmem_limit_bytes=64 * 1024 * 1024
        ),
    )(queries, key_vectors, values, query_tangent, key_tangent, value_tangent,
      frame_index, valid_counts)


def solution(mesh):
    tokens = P(("blk", "head"), None)
    return jax.shard_map(
        shards,
        mesh=mesh,
        in_specs=(tokens,) * 6 + (P("blk"), P("blk")),
        out_specs=(tokens, tokens),
        check_vma=False,
    )
```

```python
import math

import jax
import jax.numpy as jnp
from jax import lax
from jax.experimental import pallas as pl
from jax.experimental.pallas import tpu as pltpu
from jax.sharding import PartitionSpec as P

HD = 128
FRAME_TOKENS = 3600
GRID_WIDTH = 80
ROWS = 16

X, Y, ZH, ZL, C = 4, 4, 2, 4, 2
J = 3

MARK = 16384.0
MARK_FLOOR = 1000.0
MARK_WEIGHT = -1048576.0
LOW = -1.0e30

K, KT, Q, QT, V, VT = range(6)
GROUPS = ((K, 1), (KT, 1), (Q, 2), (V, 1), (VT, 1))
GROUP_OF = {K: 0, KT: 1, Q: 2, V: 3, VT: 4}
RING = (K, KT, V, VT)


def device(x, y, z, c):
    return (y * (ZH * X) + lax.div(z, ZL) * X + x, lax.rem(z, ZL) * C + c)


def nt_dot(a, b):
    return lax.dot_general(a, b, (((1,), (1,)), ((), ())), preferred_element_type=jnp.float32)


def nn_dot(a, b):
    return jnp.dot(a, b, preferred_element_type=jnp.float32)


def kernel(
    q_in, k_in, v_in, qt_in, kt_in, vt_in, frame_in, count_in,
    o_out, ot_out,
    frame_ref, count_ref, raw, send, kv, s_ref, p_ref, w_ref,
    acc_p, acc_w, acc_t, mx, mx_late, alpha, lsum, gsum, outsend, outland, final,
    small, isem, dsem, rsem, ssem, dsend, rsend, bsend, osem, osend, fsem,
):
    Z = ZH * ZL
    heads = Z * J
    span = Z * ROWS
    chunks = X * C
    near = Z // 2
    rows = Y * span
    side = rows // 2
    scale = 1.0 / math.sqrt(HD)
    scale2 = scale * math.log2(math.e)

    blk = lax.axis_index("blk")
    hd = lax.axis_index("head")
    x = lax.rem(blk, X)
    y = lax.div(blk, ZH * X)
    z = lax.rem(lax.div(blk, X), ZH) * ZL + lax.div(hd, C)
    c = lax.rem(hd, C)
    right = device(lax.rem(x + 1, X), y, z, c)
    left = device(lax.rem(x + X - 1, X), y, z, c)
    sib = device(x, y, z, 1 - c)
    own = (x * C + c) * 2
    computes = y < J

    def fetch(ref, slot):
        return pltpu.make_async_copy(ref, raw.at[slot], isem.at[slot])

    barrier = pltpu.get_barrier_semaphore()

    def greet(i, carry):
        gz = lax.rem(z + near + i, Z)
        for gy in range(Y):

            @pl.when(jnp.logical_or(gy != y, gz != z))
            def _():
                pl.semaphore_signal(barrier, inc=1, device_id=device(x, gy, gz, c))

        return carry

    lax.fori_loop(0, Z, greet, 0)
    for other in (right, left, sib):
        pl.semaphore_signal(barrier, inc=1, device_id=other)

    inputs = ((k_in, K), (kt_in, KT), (q_in, Q), (qt_in, QT), (v_in, V), (vt_in, VT))
    frames_copy = pltpu.make_async_copy(frame_in, frame_ref, small.at[0])
    counts_copy = pltpu.make_async_copy(count_in, count_ref, small.at[1])
    frames_copy.start()
    counts_copy.start()
    for ref, slot in inputs:
        fetch(ref, slot).start()

    frames_copy.wait()
    counts_copy.wait()
    row = lax.broadcasted_iota(jnp.int32, (ROWS, HD), 0)
    lane = lax.broadcasted_iota(jnp.int32, (ROWS, HD), 1)
    frame = jnp.zeros((ROWS, HD), jnp.float32)
    for i in range(ROWS):
        frame = jnp.where(row == i, frame_ref[hd * ROWS + i].astype(jnp.float32), frame)
    valid = hd * ROWS + row < count_ref[0]
    token = blk * (ROWS * ZL * C) + hd * ROWS + row
    token = jnp.where(token >= FRAME_TOKENS, token - FRAME_TOKENS, token).astype(jnp.float32)
    height = jnp.floor((token + 0.5) * (1.0 / GRID_WIDTH))
    across = token - height * GRID_WIDTH
    pair = lax.rem(lane, HD // 2)
    spatial = HD // 6
    temporal = HD // 2 - 2 * spatial
    is_frame = pair < temporal
    is_height = pair < temporal + spatial
    index = jnp.where(is_frame, pair, jnp.where(is_height, pair - temporal, pair - temporal - spatial))
    count = jnp.where(is_frame, float(temporal), float(spatial))
    freqs = jnp.exp(-math.log(10000.0) * index.astype(jnp.float32) / count)
    angles = jnp.where(is_frame, frame, jnp.where(is_height, height, across)) * freqs
    cosine = jnp.cos(angles)
    sine = jnp.sin(angles)
    sine = jnp.where(lane < HD // 2, -sine, sine)

    def rotate(ref, slot, marked=False):
        fetch(ref, slot).wait()
        for h in range(heads):
            wide = raw[slot, :, h * HD : (h + 1) * HD].astype(jnp.float32)
            turned = wide * cosine + pltpu.roll(wide, HD // 2, 1) * sine
            if marked:
                turned = jnp.where(valid, turned, MARK)
            send[h, slot] = turned.astype(jnp.bfloat16)

    def place(ref, slot):
        fetch(ref, slot).wait()
        for h in range(heads):
            send[h, slot] = raw[slot, :, h * HD : (h + 1) * HD]

    def direct(a):
        g = GROUP_OF[a]
        first, count = GROUPS[g]

        def step(i, carry):
            tz = lax.rem(z + 2 + Z - i, Z)
            u = lax.div(i, near)
            slot = lax.rem(i, near)
            for j in range(J):
                src = send.at[tz * J + j, pl.ds(first, count)]
                dst = kv.at[pl.ds(first, count), own + u, y, pl.ds(slot * ROWS, ROWS)]
                here = jnp.logical_and(tz == z, y == j)

                @pl.when(here)
                def _():
                    pltpu.make_async_copy(src, dst, dsem.at[g, u]).start()

                @pl.when(jnp.logical_not(here))
                def _():
                    pltpu.make_async_remote_copy(
                        src_ref=src, dst_ref=dst, send_sem=dsend.at[g], recv_sem=dsem.at[g, u],
                        device_id=device(x, j, tz, c),
                    ).start()

            return carry

        lax.fori_loop(0, Z, step, 0)

    def wait_direct(a, u):
        g = GROUP_OF[a]
        first, count = GROUPS[g]
        region = kv.at[pl.ds(first, count), own + u]
        pltpu.make_async_copy(region, region, dsem.at[g, u]).wait()

    def ring_send(a, part, to, event):
        n = RING.index(a)
        pltpu.make_async_remote_copy(
            src_ref=part, dst_ref=part, send_sem=rsend.at[n], recv_sem=rsem.at[n, event],
            device_id=to,
        ).start()

    def sib_send(a, part, event):
        n = RING.index(a)
        pltpu.make_async_remote_copy(
            src_ref=part, dst_ref=part, send_sem=bsend.at[n], recv_sem=ssem.at[n, event],
            device_id=sib,
        ).start()

    def origin(i):
        step = jnp.where(lax.rem(i, 2) == 0, X - 1, 1)
        sx = lax.rem(x + jnp.where(i < 2, 0, jnp.where(i < 6, step, 2)), X)
        u = jnp.where(i < 2, i, jnp.where(i < 6, lax.div(i - 2, 2), i - 6))
        return sx, u

    def places(i):
        sx, u = origin(i)
        return (sx * C + c) * 2 + u, (sx * C + 1 - c) * 2 + u

    def start(a, u):
        wait_direct(a, u)
        part = kv.at[a, own + u]
        ring_send(a, part, right, 2 + 2 * u)
        ring_send(a, part, left, 3 + 2 * u)
        sib_send(a, part, u)

    def take(a, i):
        n = RING.index(a)
        place = places(jnp.int32(i))[0]
        part = kv.at[a, place]
        halves = kv.at[a, place, pl.ds(0, Y // 2)], kv.at[a, place, pl.ds(Y // 2, Y // 2)]
        if i < 6:
            pltpu.make_async_copy(part, part, rsem.at[n, i]).wait()
            u = (i - 2) // 2
            if i % 2 == 0:
                ring_send(a, halves[0], right, 6 + 2 * u)
            else:
                ring_send(a, halves[1], left, 7 + 2 * u)
        else:
            u = i - 6
            for side_of, half in enumerate(halves):
                pltpu.make_async_copy(half, half, rsem.at[n, 6 + 2 * u + side_of]).wait()
        sib_send(a, part, i)

    def wait_sib(a, i):
        part = kv.at[a, places(i)[1]]
        pltpu.make_async_copy(part, part, ssem.at[RING.index(a), i]).wait()

    def queries_of(a):
        return kv[a, pl.ds(own, 2)].reshape(rows, HD)

    def units(a, j):
        parts = []
        for n in range(2):
            for place in places(2 * j + n):
                parts.append(kv[a, place].reshape(side, HD))
        return parts

    def wait_sibs(a, j):
        wait_sib(a, 2 * j)
        wait_sib(a, 2 * j + 1)

    def lanes(op, total, array):
        for t in range(array.shape[1] // HD):
            total = op(total, array[:, t * HD : (t + 1) * HD])
        return total

    def scores(j, top):
        wait_sibs(K, j)
        keys = units(K, j)
        last = side // Y
        marks = []
        for part in keys:
            over = jnp.maximum(part[side - last :].astype(jnp.float32) - MARK_FLOOR, 0.0)
            marks.append(jnp.zeros((side - last, HD), jnp.bfloat16))
            marks.append(over.astype(jnp.bfloat16))
        weight = jnp.full((rows, HD), MARK_WEIGHT, jnp.bfloat16)
        s = nt_dot(
            jnp.concatenate([queries_of(Q), weight], axis=1),
            jnp.concatenate([jnp.concatenate(keys, axis=0), jnp.concatenate(marks, axis=0)], axis=1),
        )
        s_ref[j] = s
        top[...] = lanes(jnp.maximum, top[...], s)

    def weights(j, top):
        wait_sibs(KT, j)
        top = jnp.concatenate([top[...]] * (2 * rows // HD), axis=1)
        p = jnp.exp2(s_ref[j] * scale2 - top)
        g = nt_dot(
            jnp.concatenate([queries_of(QT), queries_of(Q)], axis=1),
            jnp.concatenate(
                [jnp.concatenate(units(K, j), axis=0), jnp.concatenate(units(KT, j), axis=0)], axis=1
            ),
        )
        w = p * g
        lsum[...] = lanes(jnp.add, lsum[...], p)
        gsum[...] = lanes(jnp.add, gsum[...], w)
        p_ref[j] = p.astype(jnp.bfloat16)
        w_ref[j] = w.astype(jnp.bfloat16)

    def stacked(a, steps):
        parts = []
        for j in steps:
            wait_sibs(a, j)
        for j in steps:
            parts += units(a, j)
        return jnp.concatenate(parts, axis=0)

    def product(ref, steps, right_side, part=slice(None)):
        return nn_dot(jnp.concatenate([ref[j, part] for j in steps], axis=1), right_side)

    def give(which, u):
        def step(k, carry):
            tz = lax.rem(z + u * near + k + Z - 2, Z)
            for ty in range(Y):
                src = outsend.at[which, (u * Y + ty) * near + k]
                dst = outland.at[which, z * J + y]
                here = jnp.logical_and(tz == z, y == ty)

                @pl.when(here)
                def _():
                    pltpu.make_async_copy(src, dst, osem.at[which]).start()

                @pl.when(jnp.logical_not(here))
                def _():
                    pltpu.make_async_remote_copy(
                        src_ref=src, dst_ref=dst, send_sem=osend.at[which],
                        recv_sem=osem.at[which], device_id=device(x, ty, tz, c),
                    ).start()

            return carry

        lax.fori_loop(0, near, step, 0)

    def loop(work, low, high, beside=None):
        def step(i, carry):
            for k, act in (beside or {}).items():
                pl.when(i == k)(act)
            work(i)
            return carry

        lax.fori_loop(low, high, step, 0)

    def both(a, i):
        take(a, i)
        take(a, i + 1)

    rotate(k_in, K, True)
    pl.semaphore_wait(barrier, Y * Z - 1 + 3)
    direct(K)
    rotate(kt_in, KT)
    direct(KT)
    rotate(q_in, Q)
    rotate(qt_in, QT)
    direct(Q)
    place(v_in, V)
    direct(V)
    place(vt_in, VT)
    direct(VT)

    @pl.when(computes)
    def _():
        start(K, 0)
        mx[...] = jnp.full_like(mx, LOW)
        mx_late[...] = jnp.full_like(mx, LOW)
        lsum[...] = jnp.zeros_like(lsum)
        gsum[...] = jnp.zeros_like(gsum)
        start(K, 1)
        start(KT, 0)
        start(KT, 1)
        both(K, 2)
        both(K, 4)
        wait_direct(Q, 0)
        wait_direct(Q, 1)
        loop(lambda j: scores(j, mx), 0, 3, {
            1: lambda: both(KT, 2),
            2: lambda: start(V, 0),
        })
        take(K, 6)
        start(V, 1)
        both(KT, 4)
        mx[...] = jnp.broadcast_to(jnp.max(mx[...], axis=1, keepdims=True) * scale2, mx.shape)
        take(K, 7)

        def second():
            start(VT, 0)
            take(KT, 6)

        def third():
            start(VT, 1)
            both(V, 2)

        loop(lambda j: weights(j, mx), 0, 3, {1: second, 2: third})
        scores(3, mx_late)
        take(KT, 7)
        both(V, 4)
        top = jnp.maximum(mx[...], jnp.max(mx_late[...], axis=1, keepdims=True) * scale2)
        factor = jnp.exp2(mx[...] - top)
        alpha[...] = factor
        mx[...] = top
        lsum[...] = lsum[...] * factor
        gsum[...] = gsum[...] * factor
        weights(3, mx)
        both(VT, 2)
        early, middle, late = range(2), range(2, 3), range(3, 4)
        v = stacked(V, early)
        acc_p[...] = product(p_ref, early, v)
        acc_w[...] = product(w_ref, early, v)
        both(VT, 4)
        v = stacked(V, middle)
        acc_p[...] += product(p_ref, middle, v)
        acc_w[...] += product(w_ref, middle, v)
        take(V, 6)
        acc_t[...] = product(p_ref, early, stacked(VT, early))
        take(V, 7)
        v = stacked(V, late)
        inverse = 1.0 / jnp.sum(lsum[...], axis=1, keepdims=True)
        slope = jnp.sum(gsum[...], axis=1, keepdims=True) * inverse * scale
        attended = (acc_p[...] * alpha[...] + product(p_ref, late, v)) * inverse
        outsend[0] = attended.astype(jnp.bfloat16).reshape(Y * Z, ROWS, HD)
        give(0, 1)
        give(0, 0)
        acc_w[...] = (acc_w[...] * alpha[...] + product(w_ref, late, v)) * (
            inverse * scale
        ) - slope * attended
        lsum[...] = jnp.broadcast_to(inverse, lsum.shape)
        take(VT, 6)
        acc_t[...] = (acc_t[...] + product(p_ref, middle, stacked(VT, middle))) * (
            alpha[...] * lsum[...]
        ) + acc_w[...]
        take(VT, 7)
        v = stacked(VT, late)
        for u in (1, 0):
            part = slice(u * side, (u + 1) * side)
            tangent = acc_t[part] + product(p_ref, late, v, part) * lsum[part]
            outsend[1, u * Y * near : (u + 1) * Y * near] = tangent.astype(
                jnp.bfloat16
            ).reshape(Y * near, ROWS, HD)
            give(1, u)

    def finish(which, out):
        pltpu.make_async_copy(outland.at[which], outland.at[which], osem.at[which]).wait()
        for h in range(heads):
            final[which, :, h * HD : (h + 1) * HD] = outland[which, h]
        pltpu.make_async_copy(final.at[which], out, fsem.at[which]).start()

    finish(0, o_out)
    finish(1, ot_out)

    def sent(count):
        for g, (first, arrays) in enumerate(GROUPS):
            part = send.at[pl.ds(0, count), pl.ds(first, arrays)]
            pltpu.make_async_copy(part, part, dsend.at[g]).wait()

    @pl.when(computes)
    def _():
        sent(heads - 1)
        for n in range(4):
            part = kv.at[0, pl.ds(0, 6)]
            pltpu.make_async_copy(part, part, rsend.at[n]).wait()
            part = kv.at[0, pl.ds(0, 8)]
            pltpu.make_async_copy(part, part, bsend.at[n]).wait()
        for which in range(2):
            part = outsend.at[which, pl.ds(0, Y * Z - 1)]
            pltpu.make_async_copy(part, part, osend.at[which]).wait()

    @pl.when(jnp.logical_not(computes))
    def _():
        sent(heads)

    pltpu.make_async_copy(final.at[0], o_out, fsem.at[0]).wait()
    pltpu.make_async_copy(final.at[1], ot_out, fsem.at[1]).wait()


def shards(queries, key_vectors, values, query_tangent, key_tangent, value_tangent,
           frame_index, valid_counts):
    Z = ZH * ZL
    heads = Z * J
    span = Z * ROWS
    rows = Y * span
    chunks = X * C
    hbm = pl.BlockSpec(memory_space=pl.ANY)
    out = jax.ShapeDtypeStruct((ROWS, heads * HD), jnp.bfloat16)
    return pl.pallas_call(
        kernel,
        out_shape=(out, out),
        in_specs=[hbm] * 8,
        out_specs=(hbm, hbm),
        scratch_shapes=[
            pltpu.SMEM((ROWS * ZL * C,), jnp.int32),
            pltpu.SMEM((1,), jnp.int32),
            pltpu.VMEM((6, ROWS, heads * HD), jnp.bfloat16),
            pltpu.VMEM((heads, 6, ROWS, HD), jnp.bfloat16),
            pltpu.VMEM((6, chunks * 2, Y, span // 2, HD), jnp.bfloat16),
            pltpu.VMEM((chunks // 2, rows, 2 * rows), jnp.float32),
            pltpu.VMEM((chunks // 2, rows, 2 * rows), jnp.bfloat16),
            pltpu.VMEM((chunks // 2, rows, 2 * rows), jnp.bfloat16),
            pltpu.VMEM((rows, HD), jnp.float32),
            pltpu.VMEM((rows, HD), jnp.float32),
            pltpu.VMEM((rows, HD), jnp.float32),
            pltpu.VMEM((rows, HD), jnp.float32),
            pltpu.VMEM((rows, HD), jnp.float32),
            pltpu.VMEM((rows, HD), jnp.float32),
            pltpu.VMEM((rows, HD), jnp.float32),
            pltpu.VMEM((rows, HD), jnp.float32),
            pltpu.VMEM((2, Y * Z, ROWS, HD), jnp.bfloat16),
            pltpu.VMEM((2, heads, ROWS, HD), jnp.bfloat16),
            pltpu.VMEM((2, ROWS, heads * HD), jnp.bfloat16),
            pltpu.SemaphoreType.DMA((2,)),
            pltpu.SemaphoreType.DMA((6,)),
            pltpu.SemaphoreType.DMA((5, 2)),
            pltpu.SemaphoreType.DMA((4, 10)),
            pltpu.SemaphoreType.DMA((4, 8)),
            pltpu.SemaphoreType.DMA((5,)),
            pltpu.SemaphoreType.DMA((4,)),
            pltpu.SemaphoreType.DMA((4,)),
            pltpu.SemaphoreType.DMA((2,)),
            pltpu.SemaphoreType.DMA((2,)),
            pltpu.SemaphoreType.DMA((2,)),
        ],
        compiler_params=pltpu.CompilerParams(
            collective_id=0, has_side_effects=True, vmem_limit_bytes=54975 * 1024
        ),
    )(queries, key_vectors, values, query_tangent, key_tangent, value_tangent,
      frame_index, valid_counts)


def solution(mesh):
    tokens = P(("blk", "head"), None)
    return jax.shard_map(
        shards,
        mesh=mesh,
        in_specs=(tokens,) * 6 + (P("blk"), P("blk")),
        out_specs=(tokens, tokens),
        check_vma=False,
    )
```

```python
import math

import jax
import jax.numpy as jnp
from jax import lax
from jax.experimental import pallas as pl
from jax.experimental.pallas import tpu as pltpu
from jax.sharding import PartitionSpec as P

HD = 128
FRAME_TOKENS = 3600
GRID_WIDTH = 80
ROWS = 16

X, Y, ZH, ZL, C = 4, 4, 2, 4, 2
J = 3

MARK = 16384.0
MARK_FLOOR = 1000.0
MARK_WEIGHT = -1048576.0
LOW = -1.0e30

K, KT, Q, QT, V, VT = range(6)
GROUPS = ((K, 1), (KT, 1), (Q, 2), (V, 1), (VT, 1))
GROUP_OF = {K: 0, KT: 1, Q: 2, V: 3, VT: 4}
RING = (K, KT, V, VT)


def device(x, y, z, c):
    return (y * (ZH * X) + lax.div(z, ZL) * X + x, lax.rem(z, ZL) * C + c)


def nt_dot(a, b):
    return lax.dot_general(a, b, (((1,), (1,)), ((), ())), preferred_element_type=jnp.float32)


def nn_dot(a, b):
    return jnp.dot(a, b, preferred_element_type=jnp.float32)


def kernel(
    q_in, k_in, v_in, qt_in, kt_in, vt_in, frame_in, count_in,
    o_out, ot_out,
    frame_ref, count_ref, raw, send, kv, s_ref, p_ref, w_ref,
    acc_p, acc_w, acc_t, mx, mx_late, alpha, lsum, gsum, outsend,
    small, isem, dsem, rsem, ssem, dsend, rsend, bsend, osem, osend,
):
    Z = ZH * ZL
    heads = Z * J
    span = Z * ROWS
    chunks = X * C
    near = Z // 2
    rows = Y * span
    side = rows // 2
    scale = 1.0 / math.sqrt(HD)
    scale2 = scale * math.log2(math.e)

    blk = lax.axis_index("blk")
    hd = lax.axis_index("head")
    x = lax.rem(blk, X)
    y = lax.div(blk, ZH * X)
    z = lax.rem(lax.div(blk, X), ZH) * ZL + lax.div(hd, C)
    c = lax.rem(hd, C)
    right = device(lax.rem(x + 1, X), y, z, c)
    left = device(lax.rem(x + X - 1, X), y, z, c)
    sib = device(x, y, z, 1 - c)
    own = (x * C + c) * 2
    computes = y < J

    def fetch(ref, slot):
        return pltpu.make_async_copy(ref, raw.at[slot], isem.at[slot])

    frames_copy = pltpu.make_async_copy(frame_in, frame_ref, small.at[0])
    counts_copy = pltpu.make_async_copy(count_in, count_ref, small.at[1])
    frames_copy.start()
    counts_copy.start()
    fetch(k_in, K).start()

    barrier = pltpu.get_barrier_semaphore()

    def greet(i, carry):
        gz = lax.rem(z + near + i, Z)
        for gy in range(Y):

            @pl.when(jnp.logical_or(gy != y, gz != z))
            def _():
                pl.semaphore_signal(barrier, inc=1, device_id=device(x, gy, gz, c))

        return carry

    lax.fori_loop(0, Z, greet, 0)
    for other in (right, left, sib):
        pl.semaphore_signal(barrier, inc=1, device_id=other)

    for ref, slot in ((kt_in, KT), (q_in, Q), (qt_in, QT), (v_in, V), (vt_in, VT)):
        fetch(ref, slot).start()

    frames_copy.wait()
    counts_copy.wait()
    row = lax.broadcasted_iota(jnp.int32, (ROWS, HD), 0)
    lane = lax.broadcasted_iota(jnp.int32, (ROWS, HD), 1)
    frame = jnp.zeros((ROWS, HD), jnp.float32)
    for i in range(ROWS):
        frame = jnp.where(row == i, frame_ref[hd * ROWS + i].astype(jnp.float32), frame)
    valid = hd * ROWS + row < count_ref[0]
    token = blk * (ROWS * ZL * C) + hd * ROWS + row
    token = jnp.where(token >= FRAME_TOKENS, token - FRAME_TOKENS, token).astype(jnp.float32)
    height = jnp.floor((token + 0.5) * (1.0 / GRID_WIDTH))
    across = token - height * GRID_WIDTH
    pair = lax.rem(lane, HD // 2)
    spatial = HD // 6
    temporal = HD // 2 - 2 * spatial
    is_frame = pair < temporal
    is_height = pair < temporal + spatial
    index = jnp.where(is_frame, pair, jnp.where(is_height, pair - temporal, pair - temporal - spatial))
    count = jnp.where(is_frame, float(temporal), float(spatial))
    freqs = jnp.exp(-math.log(10000.0) * index.astype(jnp.float32) / count)
    angles = jnp.where(is_frame, frame, jnp.where(is_height, height, across)) * freqs
    cosine = jnp.cos(angles)
    sine = jnp.sin(angles)
    sine = jnp.where(lane < HD // 2, -sine, sine)

    def rotate(ref, slot, marked=False):
        fetch(ref, slot).wait()
        for h in range(heads):
            wide = raw[slot, :, h * HD : (h + 1) * HD].astype(jnp.float32)
            turned = wide * cosine + pltpu.roll(wide, HD // 2, 1) * sine
            if marked:
                turned = jnp.where(valid, turned, MARK)
            send[h, slot] = turned.astype(jnp.bfloat16)

    def place(ref, slot):
        fetch(ref, slot).wait()
        for h in range(heads):
            send[h, slot] = raw[slot, :, h * HD : (h + 1) * HD]

    def direct(a):
        g = GROUP_OF[a]
        first, count = GROUPS[g]

        def step(i, carry):
            tz = lax.rem(z + 2 + Z - i, Z)
            u = lax.div(i, near)
            slot = lax.rem(i, near)
            for j in range(J):
                src = send.at[tz * J + j, pl.ds(first, count)]
                dst = kv.at[pl.ds(first, count), own + u, y, pl.ds(slot * ROWS, ROWS)]
                here = jnp.logical_and(tz == z, y == j)

                @pl.when(here)
                def _():
                    pltpu.make_async_copy(src, dst, dsem.at[g, u]).start()

                @pl.when(jnp.logical_not(here))
                def _():
                    pltpu.make_async_remote_copy(
                        src_ref=src, dst_ref=dst, send_sem=dsend.at[g], recv_sem=dsem.at[g, u],
                        device_id=device(x, j, tz, c),
                    ).start()

            return carry

        lax.fori_loop(0, Z, step, 0)

    def wait_direct(a, u):
        g = GROUP_OF[a]
        first, count = GROUPS[g]
        region = kv.at[pl.ds(first, count), own + u]
        pltpu.make_async_copy(region, region, dsem.at[g, u]).wait()

    def ring_send(a, part, to, event):
        n = RING.index(a)
        pltpu.make_async_remote_copy(
            src_ref=part, dst_ref=part, send_sem=rsend.at[n], recv_sem=rsem.at[n, event],
            device_id=to,
        ).start()

    def sib_send(a, part, event):
        n = RING.index(a)
        pltpu.make_async_remote_copy(
            src_ref=part, dst_ref=part, send_sem=bsend.at[n], recv_sem=ssem.at[n, event],
            device_id=sib,
        ).start()

    def origin(i):
        step = jnp.where(lax.rem(i, 2) == 0, X - 1, 1)
        sx = lax.rem(x + jnp.where(i < 2, 0, jnp.where(i < 6, step, 2)), X)
        u = jnp.where(i < 2, i, jnp.where(i < 6, lax.div(i - 2, 2), i - 6))
        return sx, u

    def places(i):
        sx, u = origin(i)
        return (sx * C + c) * 2 + u, (sx * C + 1 - c) * 2 + u

    def start(a, u):
        wait_direct(a, u)
        part = kv.at[a, own + u]
        ring_send(a, part, right, 2 + 2 * u)
        ring_send(a, part, left, 3 + 2 * u)
        sib_send(a, part, u)

    def take(a, i):
        n = RING.index(a)
        place = places(jnp.int32(i))[0]
        part = kv.at[a, place]
        halves = kv.at[a, place, pl.ds(0, Y // 2)], kv.at[a, place, pl.ds(Y // 2, Y // 2)]
        if i < 6:
            pltpu.make_async_copy(part, part, rsem.at[n, i]).wait()
            u = (i - 2) // 2
            if i % 2 == 0:
                ring_send(a, halves[0], right, 6 + 2 * u)
            else:
                ring_send(a, halves[1], left, 7 + 2 * u)
        else:
            u = i - 6
            for side_of, half in enumerate(halves):
                pltpu.make_async_copy(half, half, rsem.at[n, 6 + 2 * u + side_of]).wait()
        sib_send(a, part, i)

    def wait_sib(a, i):
        part = kv.at[a, places(i)[1]]
        pltpu.make_async_copy(part, part, ssem.at[RING.index(a), i]).wait()

    def queries_of(a):
        return kv[a, pl.ds(own, 2)].reshape(rows, HD)

    def units(a, j):
        parts = []
        for n in range(2):
            for place in places(2 * j + n):
                parts.append(kv[a, place].reshape(side, HD))
        return parts

    def wait_sibs(a, j):
        wait_sib(a, 2 * j)
        wait_sib(a, 2 * j + 1)

    def lanes(op, total, array):
        for t in range(array.shape[1] // HD):
            total = op(total, array[:, t * HD : (t + 1) * HD])
        return total

    def scores(j, top):
        wait_sibs(K, j)
        keys = units(K, j)
        last = side // Y
        marks = []
        for part in keys:
            over = jnp.maximum(part[side - last :].astype(jnp.float32) - MARK_FLOOR, 0.0)
            marks.append(jnp.zeros((side - last, HD), jnp.bfloat16))
            marks.append(over.astype(jnp.bfloat16))
        weight = jnp.full((rows, HD), MARK_WEIGHT, jnp.bfloat16)
        s = nt_dot(
            jnp.concatenate([queries_of(Q), weight], axis=1),
            jnp.concatenate([jnp.concatenate(keys, axis=0), jnp.concatenate(marks, axis=0)], axis=1),
        )
        s_ref[j] = s
        top[...] = lanes(jnp.maximum, top[...], s)

    def weights(j, top):
        wait_sibs(KT, j)
        top = jnp.concatenate([top[...]] * (2 * rows // HD), axis=1)
        p = jnp.exp2(s_ref[j] * scale2 - top)
        g = nt_dot(
            jnp.concatenate([queries_of(QT), queries_of(Q)], axis=1),
            jnp.concatenate(
                [jnp.concatenate(units(K, j), axis=0), jnp.concatenate(units(KT, j), axis=0)], axis=1
            ),
        )
        w = p * g
        lsum[...] = lanes(jnp.add, lsum[...], p)
        gsum[...] = lanes(jnp.add, gsum[...], w)
        p_ref[j] = p.astype(jnp.bfloat16)
        w_ref[j] = w.astype(jnp.bfloat16)

    def stacked(a, steps):
        parts = []
        for j in steps:
            wait_sibs(a, j)
        for j in steps:
            parts += units(a, j)
        return jnp.concatenate(parts, axis=0)

    def product(ref, steps, right_side, part=slice(None)):
        return nn_dot(jnp.concatenate([ref[j, part] for j in steps], axis=1), right_side)

    def give(which, u):
        out = (o_out, ot_out)[which]

        def step(k, carry):
            tz = lax.rem(z + u * near + k + Z - 2, Z)
            for ty in range(Y):
                src = outsend.at[which, (u * Y + ty) * near + k]
                dst = out.at[:, pl.ds(pl.multiple_of((z * J + y) * HD, HD), HD)]
                here = jnp.logical_and(tz == z, y == ty)

                @pl.when(here)
                def _():
                    pltpu.make_async_copy(src, dst, osem.at[which]).start()

                @pl.when(jnp.logical_not(here))
                def _():
                    pltpu.make_async_remote_copy(
                        src_ref=src, dst_ref=dst, send_sem=osend.at[which],
                        recv_sem=osem.at[which], device_id=device(x, ty, tz, c),
                    ).start()

            return carry

        lax.fori_loop(0, near, step, 0)

    def loop(work, low, high, beside=None):
        def step(i, carry):
            for k, act in (beside or {}).items():
                pl.when(i == k)(act)
            work(i)
            return carry

        lax.fori_loop(low, high, step, 0)

    def both(a, i):
        take(a, i)
        take(a, i + 1)

    rotate(k_in, K, True)
    pl.semaphore_wait(barrier, Y * Z - 1 + 3)
    direct(K)
    rotate(kt_in, KT)
    direct(KT)
    rotate(q_in, Q)
    rotate(qt_in, QT)
    direct(Q)
    place(v_in, V)
    direct(V)
    place(vt_in, VT)
    direct(VT)

    @pl.when(computes)
    def _():
        start(K, 0)
        mx[...] = jnp.full_like(mx, LOW)
        mx_late[...] = jnp.full_like(mx, LOW)
        lsum[...] = jnp.zeros_like(lsum)
        gsum[...] = jnp.zeros_like(gsum)
        start(K, 1)
        start(KT, 0)
        start(KT, 1)
        both(K, 2)
        both(K, 4)
        wait_direct(Q, 0)
        wait_direct(Q, 1)
        loop(lambda j: scores(j, mx), 0, 3, {
            1: lambda: both(KT, 2),
            2: lambda: start(V, 0),
        })
        take(K, 6)
        start(V, 1)
        both(KT, 4)
        mx[...] = jnp.broadcast_to(jnp.max(mx[...], axis=1, keepdims=True) * scale2, mx.shape)
        take(K, 7)

        def second():
            start(VT, 0)
            take(KT, 6)

        def third():
            start(VT, 1)
            both(V, 2)

        loop(lambda j: weights(j, mx), 0, 3, {1: second, 2: third})
        scores(3, mx_late)
        take(KT, 7)
        both(V, 4)
        early, middle, late = range(2), range(2, 3), range(3, 4)
        v = stacked(V, early)
        acc_p[...] = product(p_ref, early, v)
        acc_w[...] = product(w_ref, early, v)
        both(VT, 2)
        top = jnp.maximum(mx[...], jnp.max(mx_late[...], axis=1, keepdims=True) * scale2)
        factor = jnp.exp2(mx[...] - top)
        alpha[...] = factor
        mx[...] = top
        lsum[...] = lsum[...] * factor
        gsum[...] = gsum[...] * factor
        weights(3, mx)
        both(VT, 4)
        v = stacked(V, middle)
        acc_p[...] += product(p_ref, middle, v)
        acc_w[...] += product(w_ref, middle, v)
        take(V, 6)
        acc_t[...] = product(p_ref, early, stacked(VT, early))
        take(V, 7)
        acc_t[...] += product(p_ref, middle, stacked(VT, middle))
        v = stacked(V, late)
        inverse = 1.0 / jnp.sum(lsum[...], axis=1, keepdims=True)
        slope = jnp.sum(gsum[...], axis=1, keepdims=True) * inverse * scale
        attended = (acc_p[...] * alpha[...] + product(p_ref, late, v)) * inverse
        outsend[0] = attended.astype(jnp.bfloat16).reshape(Y * Z, ROWS, HD)
        both(VT, 6)
        give(0, 1)
        give(0, 0)
        acc_w[...] = (acc_w[...] * alpha[...] + product(w_ref, late, v)) * (
            inverse * scale
        ) - slope * attended
        lsum[...] = jnp.broadcast_to(inverse, lsum.shape)
        acc_t[...] = acc_t[...] * (alpha[...] * lsum[...]) + acc_w[...]
        v = stacked(VT, late)
        for u in (1, 0):
            part = slice(u * side, (u + 1) * side)
            tangent = acc_t[part] + product(p_ref, late, v, part) * lsum[part]
            outsend[1, u * Y * near : (u + 1) * Y * near] = tangent.astype(
                jnp.bfloat16
            ).reshape(Y * near, ROWS, HD)
            give(1, u)

    for which, out in ((0, o_out), (1, ot_out)):
        pltpu.make_async_copy(out, out, osem.at[which]).wait()

    def sent(count):
        for g, (first, arrays) in enumerate(GROUPS):
            part = send.at[pl.ds(0, count), pl.ds(first, arrays)]
            pltpu.make_async_copy(part, part, dsend.at[g]).wait()

    @pl.when(computes)
    def _():
        sent(heads - 1)
        for n in range(4):
            part = kv.at[0, pl.ds(0, 6)]
            pltpu.make_async_copy(part, part, rsend.at[n]).wait()
            part = kv.at[0, pl.ds(0, 8)]
            pltpu.make_async_copy(part, part, bsend.at[n]).wait()
        for which in range(2):
            part = outsend.at[which, pl.ds(0, Y * Z - 1)]
            pltpu.make_async_copy(part, part, osend.at[which]).wait()

    @pl.when(jnp.logical_not(computes))
    def _():
        sent(heads)


def shards(queries, key_vectors, values, query_tangent, key_tangent, value_tangent,
           frame_index, valid_counts):
    Z = ZH * ZL
    heads = Z * J
    span = Z * ROWS
    rows = Y * span
    chunks = X * C
    hbm = pl.BlockSpec(memory_space=pl.ANY)
    out = jax.ShapeDtypeStruct((ROWS, heads * HD), jnp.bfloat16)
    return pl.pallas_call(
        kernel,
        out_shape=(out, out),
        in_specs=[hbm] * 8,
        out_specs=(hbm, hbm),
        scratch_shapes=[
            pltpu.SMEM((ROWS * ZL * C,), jnp.int32),
            pltpu.SMEM((1,), jnp.int32),
            pltpu.VMEM((6, ROWS, heads * HD), jnp.bfloat16),
            pltpu.VMEM((heads, 6, ROWS, HD), jnp.bfloat16),
            pltpu.VMEM((6, chunks * 2, Y, span // 2, HD), jnp.bfloat16),
            pltpu.VMEM((chunks // 2, rows, 2 * rows), jnp.float32),
            pltpu.VMEM((chunks // 2, rows, 2 * rows), jnp.bfloat16),
            pltpu.VMEM((chunks // 2, rows, 2 * rows), jnp.bfloat16),
            pltpu.VMEM((rows, HD), jnp.float32),
            pltpu.VMEM((rows, HD), jnp.float32),
            pltpu.VMEM((rows, HD), jnp.float32),
            pltpu.VMEM((rows, HD), jnp.float32),
            pltpu.VMEM((rows, HD), jnp.float32),
            pltpu.VMEM((rows, HD), jnp.float32),
            pltpu.VMEM((rows, HD), jnp.float32),
            pltpu.VMEM((rows, HD), jnp.float32),
            pltpu.VMEM((2, Y * Z, ROWS, HD), jnp.bfloat16),
            pltpu.SemaphoreType.DMA((2,)),
            pltpu.SemaphoreType.DMA((6,)),
            pltpu.SemaphoreType.DMA((5, 2)),
            pltpu.SemaphoreType.DMA((4, 10)),
            pltpu.SemaphoreType.DMA((4, 8)),
            pltpu.SemaphoreType.DMA((5,)),
            pltpu.SemaphoreType.DMA((4,)),
            pltpu.SemaphoreType.DMA((4,)),
            pltpu.SemaphoreType.DMA((2,)),
            pltpu.SemaphoreType.DMA((2,)),
        ],
        compiler_params=pltpu.CompilerParams(
            collective_id=0, has_side_effects=True, vmem_limit_bytes=54975 * 1024
        ),
    )(queries, key_vectors, values, query_tangent, key_tangent, value_tangent,
      frame_index, valid_counts)


def solution(mesh):
    tokens = P(("blk", "head"), None)
    return jax.shard_map(
        shards,
        mesh=mesh,
        in_specs=(tokens,) * 6 + (P("blk"), P("blk")),
        out_specs=(tokens, tokens),
        check_vma=False,
    )
```

```python
import math

import jax
import jax.numpy as jnp
from jax import lax
from jax.experimental import pallas as pl
from jax.experimental.pallas import tpu as pltpu
from jax.sharding import PartitionSpec as P

HD = 128
FRAME_TOKENS = 3600
GRID_WIDTH = 80
ROWS = 16

X, Y, ZH, ZL, C = 4, 4, 2, 4, 2
J = 3

MARK = 16384.0
MARK_FLOOR = 1000.0
MARK_WEIGHT = -1048576.0
LOW = -1.0e30

K, KT, Q, QT, V, VT = range(6)
GROUPS = ((K, 1), (KT, 1), (Q, 2), (V, 1), (VT, 1))
GROUP_OF = {K: 0, KT: 1, Q: 2, V: 3, VT: 4}
RING = (K, KT, V, VT)
RELAYED = (KT,)


def device(x, y, z, c):
    return (y * (ZH * X) + lax.div(z, ZL) * X + x, lax.rem(z, ZL) * C + c)


def nt_dot(a, b):
    return lax.dot_general(a, b, (((1,), (1,)), ((), ())), preferred_element_type=jnp.float32)


def nn_dot(a, b):
    return jnp.dot(a, b, preferred_element_type=jnp.float32)


def kernel(
    q_in, k_in, v_in, qt_in, kt_in, vt_in, frame_in, count_in,
    o_out, ot_out,
    frame_ref, count_ref, raw, send, kv, s_ref, p_ref, w_ref,
    acc_p, acc_w, acc_t, mx, mx_late, alpha, lsum, gsum, outsend, passing,
    small, isem, dsem, rsem, ssem, dsend, rsend, bsend, osem, osend, psem, psend,
):
    Z = ZH * ZL
    heads = Z * J
    span = Z * ROWS
    chunks = X * C
    near = Z // 2
    rows = Y * span
    side = rows // 2
    scale = 1.0 / math.sqrt(HD)
    scale2 = scale * math.log2(math.e)

    blk = lax.axis_index("blk")
    hd = lax.axis_index("head")
    x = lax.rem(blk, X)
    y = lax.div(blk, ZH * X)
    z = lax.rem(lax.div(blk, X), ZH) * ZL + lax.div(hd, C)
    c = lax.rem(hd, C)
    right = device(lax.rem(x + 1, X), y, z, c)
    left = device(lax.rem(x + X - 1, X), y, z, c)
    sib = device(x, y, z, 1 - c)
    across_x = lax.rem(x + 2, X)
    relay = device(x, Y - 1, z, c)
    own = (x * C + c) * 2
    computes = y < J

    def fetch(ref, slot):
        return pltpu.make_async_copy(ref, raw.at[slot], isem.at[slot])

    frames_copy = pltpu.make_async_copy(frame_in, frame_ref, small.at[0])
    counts_copy = pltpu.make_async_copy(count_in, count_ref, small.at[1])
    frames_copy.start()
    counts_copy.start()
    fetch(k_in, K).start()

    barrier = pltpu.get_barrier_semaphore()

    def greet(i, carry):
        gz = lax.rem(z + near + i, Z)
        for gy in range(Y):

            @pl.when(jnp.logical_or(gy != y, gz != z))
            def _():
                pl.semaphore_signal(barrier, inc=1, device_id=device(x, gy, gz, c))

        return carry

    lax.fori_loop(0, Z, greet, 0)
    for other in (right, left, sib):
        pl.semaphore_signal(barrier, inc=1, device_id=other)

    @pl.when(computes)
    def _():
        pl.semaphore_signal(barrier, inc=1, device_id=device(across_x, Y - 1, z, c))

    @pl.when(jnp.logical_not(computes))
    def _():
        for j in range(J):
            pl.semaphore_signal(barrier, inc=1, device_id=device(across_x, j, z, c))


    for ref, slot in ((kt_in, KT), (q_in, Q), (qt_in, QT), (v_in, V), (vt_in, VT)):
        fetch(ref, slot).start()

    frames_copy.wait()
    counts_copy.wait()
    row = lax.broadcasted_iota(jnp.int32, (ROWS, HD), 0)
    lane = lax.broadcasted_iota(jnp.int32, (ROWS, HD), 1)
    frame = jnp.zeros((ROWS, HD), jnp.float32)
    for i in range(ROWS):
        frame = jnp.where(row == i, frame_ref[hd * ROWS + i].astype(jnp.float32), frame)
    valid = hd * ROWS + row < count_ref[0]
    token = blk * (ROWS * ZL * C) + hd * ROWS + row
    token = jnp.where(token >= FRAME_TOKENS, token - FRAME_TOKENS, token).astype(jnp.float32)
    height = jnp.floor((token + 0.5) * (1.0 / GRID_WIDTH))
    across = token - height * GRID_WIDTH
    pair = lax.rem(lane, HD // 2)
    spatial = HD // 6
    temporal = HD // 2 - 2 * spatial
    is_frame = pair < temporal
    is_height = pair < temporal + spatial
    index = jnp.where(is_frame, pair, jnp.where(is_height, pair - temporal, pair - temporal - spatial))
    count = jnp.where(is_frame, float(temporal), float(spatial))
    freqs = jnp.exp(-math.log(10000.0) * index.astype(jnp.float32) / count)
    angles = jnp.where(is_frame, frame, jnp.where(is_height, height, across)) * freqs
    cosine = jnp.cos(angles)
    sine = jnp.sin(angles)
    sine = jnp.where(lane < HD // 2, -sine, sine)

    def rotate(ref, slot, marked=False):
        fetch(ref, slot).wait()
        for h in range(heads):
            wide = raw[slot, :, h * HD : (h + 1) * HD].astype(jnp.float32)
            turned = wide * cosine + pltpu.roll(wide, HD // 2, 1) * sine
            if marked:
                turned = jnp.where(valid, turned, MARK)
            send[h, slot] = turned.astype(jnp.bfloat16)

    def place(ref, slot):
        fetch(ref, slot).wait()
        for h in range(heads):
            send[h, slot] = raw[slot, :, h * HD : (h + 1) * HD]

    def direct(a):
        g = GROUP_OF[a]
        first, count = GROUPS[g]

        def step(i, carry):
            tz = lax.rem(z + 2 + Z - i, Z)
            u = lax.div(i, near)
            slot = lax.rem(i, near)
            for j in range(J):
                src = send.at[tz * J + j, pl.ds(first, count)]
                dst = kv.at[pl.ds(first, count), own + u, y, pl.ds(slot * ROWS, ROWS)]
                here = jnp.logical_and(tz == z, y == j)

                @pl.when(here)
                def _():
                    pltpu.make_async_copy(src, dst, dsem.at[g, u]).start()

                @pl.when(jnp.logical_not(here))
                def _():
                    pltpu.make_async_remote_copy(
                        src_ref=src, dst_ref=dst, send_sem=dsend.at[g], recv_sem=dsem.at[g, u],
                        device_id=device(x, j, tz, c),
                    ).start()

            return carry

        lax.fori_loop(0, Z, step, 0)

    def wait_direct(a, u):
        g = GROUP_OF[a]
        first, count = GROUPS[g]
        region = kv.at[pl.ds(first, count), own + u]
        pltpu.make_async_copy(region, region, dsem.at[g, u]).wait()

    def ring_send(a, part, to, event):
        n = RING.index(a)
        pltpu.make_async_remote_copy(
            src_ref=part, dst_ref=part, send_sem=rsend.at[n], recv_sem=rsem.at[n, event],
            device_id=to,
        ).start()

    def sib_send(a, part, event):
        n = RING.index(a)
        pltpu.make_async_remote_copy(
            src_ref=part, dst_ref=part, send_sem=bsend.at[n], recv_sem=ssem.at[n, event],
            device_id=sib,
        ).start()

    def origin(i):
        step = jnp.where(lax.rem(i, 2) == 0, X - 1, 1)
        sx = lax.rem(x + jnp.where(i < 2, 0, jnp.where(i < 6, step, 2)), X)
        u = jnp.where(i < 2, i, jnp.where(i < 6, lax.div(i - 2, 2), i - 6))
        return sx, u

    def places(i):
        sx, u = origin(i)
        return (sx * C + c) * 2 + u, (sx * C + 1 - c) * 2 + u

    def start(a, u):
        wait_direct(a, u)
        part = kv.at[a, own + u]
        ring_send(a, part, right, u)
        ring_send(a, part, left, u)
        if a in RELAYED and u == 1:
            r = RELAYED.index(a)
            pltpu.make_async_remote_copy(
                src_ref=part, dst_ref=passing.at[r, y], send_sem=rsend.at[RING.index(a)],
                recv_sem=psem.at[r, y], device_id=relay,
            ).start()
        sib_send(a, part, 0)

    def arrived(sem, units_of):
        part = kv.at[0, pl.ds(0, units_of)]
        pltpu.make_async_copy(part, part, sem).wait()

    def unit_halves(a, i):
        place = places(jnp.int32(i))[0]
        half = Y // 2
        return kv.at[a, place], kv.at[a, place, pl.ds(0, half)], kv.at[a, place, pl.ds(half, half)]

    def neighbours(a, u):
        arrived(rsem.at[RING.index(a), u], 2)
        from_left, first, _ = unit_halves(a, 2 + 2 * u)
        from_right, _, second = unit_halves(a, 3 + 2 * u)
        if a not in RELAYED or u == 0:
            ring_send(a, first, right, 2 + u)
            ring_send(a, second, left, 2 + u)
        sib_send(a, from_left, 1 + u)
        sib_send(a, from_right, 1 + u)

    def opposite(a, u):
        arrived(rsem.at[RING.index(a), 2 + u], 1)
        sib_send(a, unit_halves(a, 6 + u)[0], 3)

    def wait_sibs(a, j):
        arrived(ssem.at[RING.index(a), j], 2)

    def queries_of(a):
        return kv[a, pl.ds(own, 2)].reshape(rows, HD)

    def units(a, j):
        parts = []
        for n in range(2):
            for place in places(2 * j + n):
                parts.append(kv[a, place].reshape(side, HD))
        return parts

    def lanes(op, total, array):
        for t in range(array.shape[1] // HD):
            total = op(total, array[:, t * HD : (t + 1) * HD])
        return total

    def scores(j, top):
        wait_sibs(K, j)
        keys = units(K, j)
        last = side // Y
        marks = []
        for part in keys:
            over = jnp.maximum(part[side - last :].astype(jnp.float32) - MARK_FLOOR, 0.0)
            marks.append(jnp.zeros((side - last, HD), jnp.bfloat16))
            marks.append(over.astype(jnp.bfloat16))
        weight = jnp.full((rows, HD), MARK_WEIGHT, jnp.bfloat16)
        s = nt_dot(
            jnp.concatenate([queries_of(Q), weight], axis=1),
            jnp.concatenate([jnp.concatenate(keys, axis=0), jnp.concatenate(marks, axis=0)], axis=1),
        )
        s_ref[j] = s
        top[...] = lanes(jnp.maximum, top[...], s)

    def weights(j, top):
        wait_sibs(KT, j)
        top = jnp.concatenate([top[...]] * (2 * rows // HD), axis=1)
        p = jnp.exp2(s_ref[j] * scale2 - top)
        g = nt_dot(
            jnp.concatenate([queries_of(QT), queries_of(Q)], axis=1),
            jnp.concatenate(
                [jnp.concatenate(units(K, j), axis=0), jnp.concatenate(units(KT, j), axis=0)], axis=1
            ),
        )
        w = p * g
        lsum[...] = lanes(jnp.add, lsum[...], p)
        gsum[...] = lanes(jnp.add, gsum[...], w)
        p_ref[j] = p.astype(jnp.bfloat16)
        w_ref[j] = w.astype(jnp.bfloat16)

    def stacked(a, steps):
        parts = []
        for j in steps:
            wait_sibs(a, j)
        for j in steps:
            parts += units(a, j)
        return jnp.concatenate(parts, axis=0)

    def product(ref, steps, right_side, part=slice(None)):
        return nn_dot(jnp.concatenate([ref[j, part] for j in steps], axis=1), right_side)

    def give(which, u):
        out = (o_out, ot_out)[which]

        def step(k, carry):
            tz = lax.rem(z + u * near + k + Z - 2, Z)
            for ty in range(Y):
                src = outsend.at[which, (u * Y + ty) * near + k]
                dst = out.at[:, pl.ds(pl.multiple_of((z * J + y) * HD, HD), HD)]
                here = jnp.logical_and(tz == z, y == ty)

                @pl.when(here)
                def _():
                    pltpu.make_async_copy(src, dst, osem.at[which]).start()

                @pl.when(jnp.logical_not(here))
                def _():
                    pltpu.make_async_remote_copy(
                        src_ref=src, dst_ref=dst, send_sem=osend.at[which],
                        recv_sem=osem.at[which], device_id=device(x, ty, tz, c),
                    ).start()

            return carry

        lax.fori_loop(0, near, step, 0)

    def loop(work, low, high, beside=None):
        def step(i, carry):
            for k, act in (beside or {}).items():
                pl.when(i == k)(act)
            work(i)
            return carry

        lax.fori_loop(low, high, step, 0)

    rotate(k_in, K, True)
    pl.semaphore_wait(barrier, Y * Z - 1 + 3 + jnp.where(computes, 1, J))
    direct(K)
    rotate(kt_in, KT)
    direct(KT)
    rotate(q_in, Q)
    rotate(qt_in, QT)
    direct(Q)
    place(v_in, V)
    direct(V)
    place(vt_in, VT)
    direct(VT)

    @pl.when(computes)
    def _():
        start(K, 0)
        mx[...] = jnp.full_like(mx, LOW)
        mx_late[...] = jnp.full_like(mx, LOW)
        lsum[...] = jnp.zeros_like(lsum)
        gsum[...] = jnp.zeros_like(gsum)
        start(K, 1)
        start(KT, 0)
        start(KT, 1)
        neighbours(K, 0)
        neighbours(K, 1)
        wait_direct(Q, 0)
        wait_direct(Q, 1)
        loop(lambda j: scores(j, mx), 0, 3, {
            1: lambda: neighbours(KT, 0),
            2: lambda: start(V, 0),
        })
        opposite(K, 0)
        start(V, 1)
        neighbours(KT, 1)
        mx[...] = jnp.broadcast_to(jnp.max(mx[...], axis=1, keepdims=True) * scale2, mx.shape)
        opposite(K, 1)

        def second():
            start(VT, 0)
            opposite(KT, 0)

        def third():
            start(VT, 1)
            neighbours(V, 0)

        loop(lambda j: weights(j, mx), 0, 3, {1: second, 2: third})
        scores(3, mx_late)
        opposite(KT, 1)
        neighbours(V, 1)
        early, middle, late = range(2), range(2, 3), range(3, 4)
        v = stacked(V, early)
        acc_p[...] = product(p_ref, early, v)
        acc_w[...] = product(w_ref, early, v)
        neighbours(VT, 0)
        top = jnp.maximum(mx[...], jnp.max(mx_late[...], axis=1, keepdims=True) * scale2)
        factor = jnp.exp2(mx[...] - top)
        alpha[...] = factor
        mx[...] = top
        lsum[...] = lsum[...] * factor
        gsum[...] = gsum[...] * factor
        weights(3, mx)
        neighbours(VT, 1)
        v = stacked(V, middle)
        acc_p[...] += product(p_ref, middle, v)
        acc_w[...] += product(w_ref, middle, v)
        opposite(V, 0)
        acc_t[...] = product(p_ref, early, stacked(VT, early))
        opposite(V, 1)
        acc_t[...] += product(p_ref, middle, stacked(VT, middle))
        v = stacked(V, late)
        inverse = 1.0 / jnp.sum(lsum[...], axis=1, keepdims=True)
        slope = jnp.sum(gsum[...], axis=1, keepdims=True) * inverse * scale
        attended = (acc_p[...] * alpha[...] + product(p_ref, late, v)) * inverse
        outsend[0] = attended.astype(jnp.bfloat16).reshape(Y * Z, ROWS, HD)
        give(0, 1)
        give(0, 0)
        opposite(VT, 0)
        opposite(VT, 1)
        acc_w[...] = (acc_w[...] * alpha[...] + product(w_ref, late, v)) * (
            inverse * scale
        ) - slope * attended
        lsum[...] = jnp.broadcast_to(inverse, lsum.shape)
        acc_t[...] = acc_t[...] * (alpha[...] * lsum[...]) + acc_w[...]
        v = stacked(VT, late)
        for u in (1, 0):
            part = slice(u * side, (u + 1) * side)
            tangent = acc_t[part] + product(p_ref, late, v, part) * lsum[part]
            outsend[1, u * Y * near : (u + 1) * Y * near] = tangent.astype(
                jnp.bfloat16
            ).reshape(Y * near, ROWS, HD)
            give(1, u)

    @pl.when(jnp.logical_not(computes))
    def _():
        for r, a in enumerate(RELAYED):
            for j in range(J):
                part = passing.at[r, j]
                pltpu.make_async_copy(part, part, psem.at[r, j]).wait()
                pltpu.make_async_remote_copy(
                    src_ref=part, dst_ref=kv.at[a, own + 1], send_sem=psend,
                    recv_sem=rsem.at[RING.index(a), 3], device_id=device(across_x, j, z, c),
                ).start()

    for which, out in ((0, o_out), (1, ot_out)):
        pltpu.make_async_copy(out, out, osem.at[which]).wait()

    def sent(count):
        for g, (first, arrays) in enumerate(GROUPS):
            part = send.at[pl.ds(0, count), pl.ds(first, arrays)]
            pltpu.make_async_copy(part, part, dsend.at[g]).wait()

    @pl.when(computes)
    def _():
        sent(heads - 1)
        for n in range(4):
            part = kv.at[0, pl.ds(0, 6)]
            pltpu.make_async_copy(part, part, rsend.at[n]).wait()
            part = kv.at[0, pl.ds(0, 8)]
            pltpu.make_async_copy(part, part, bsend.at[n]).wait()
        for which in range(2):
            part = outsend.at[which, pl.ds(0, Y * Z - 1)]
            pltpu.make_async_copy(part, part, osend.at[which]).wait()

    @pl.when(jnp.logical_not(computes))
    def _():
        sent(heads)
        arrived(psend, len(RELAYED) * J)


def shards(queries, key_vectors, values, query_tangent, key_tangent, value_tangent,
           frame_index, valid_counts):
    Z = ZH * ZL
    heads = Z * J
    span = Z * ROWS
    rows = Y * span
    chunks = X * C
    hbm = pl.BlockSpec(memory_space=pl.ANY)
    out = jax.ShapeDtypeStruct((ROWS, heads * HD), jnp.bfloat16)
    return pl.pallas_call(
        kernel,
        out_shape=(out, out),
        in_specs=[hbm] * 8,
        out_specs=(hbm, hbm),
        scratch_shapes=[
            pltpu.SMEM((ROWS * ZL * C,), jnp.int32),
            pltpu.SMEM((1,), jnp.int32),
            pltpu.VMEM((6, ROWS, heads * HD), jnp.bfloat16),
            pltpu.VMEM((heads, 6, ROWS, HD), jnp.bfloat16),
            pltpu.VMEM((6, chunks * 2, Y, span // 2, HD), jnp.bfloat16),
            pltpu.VMEM((chunks // 2, rows, 2 * rows), jnp.float32),
            pltpu.VMEM((chunks // 2, rows, 2 * rows), jnp.bfloat16),
            pltpu.VMEM((chunks // 2, rows, 2 * rows), jnp.bfloat16),
            pltpu.VMEM((rows, HD), jnp.float32),
            pltpu.VMEM((rows, HD), jnp.float32),
            pltpu.VMEM((rows, HD), jnp.float32),
            pltpu.VMEM((rows, HD), jnp.float32),
            pltpu.VMEM((rows, HD), jnp.float32),
            pltpu.VMEM((rows, HD), jnp.float32),
            pltpu.VMEM((rows, HD), jnp.float32),
            pltpu.VMEM((rows, HD), jnp.float32),
            pltpu.VMEM((2, Y * Z, ROWS, HD), jnp.bfloat16),
            pltpu.VMEM((len(RELAYED), J, Y, span // 2, HD), jnp.bfloat16),
            pltpu.SemaphoreType.DMA((2,)),
            pltpu.SemaphoreType.DMA((6,)),
            pltpu.SemaphoreType.DMA((5, 2)),
            pltpu.SemaphoreType.DMA((4, 4)),
            pltpu.SemaphoreType.DMA((4, 4)),
            pltpu.SemaphoreType.DMA((5,)),
            pltpu.SemaphoreType.DMA((4,)),
            pltpu.SemaphoreType.DMA((4,)),
            pltpu.SemaphoreType.DMA((2,)),
            pltpu.SemaphoreType.DMA((2,)),
            pltpu.SemaphoreType.DMA((len(RELAYED), J)),
            pltpu.SemaphoreType.DMA,
        ],
        compiler_params=pltpu.CompilerParams(
            collective_id=0, has_side_effects=True, vmem_limit_bytes=54975 * 1024
        ),
    )(queries, key_vectors, values, query_tangent, key_tangent, value_tangent,
      frame_index, valid_counts)


def solution(mesh):
    tokens = P(("blk", "head"), None)
    return jax.shard_map(
        shards,
        mesh=mesh,
        in_specs=(tokens,) * 6 + (P("blk"), P("blk")),
        out_specs=(tokens, tokens),
        check_vma=False,
    )
```

```python
import math

import jax
import jax.numpy as jnp
from jax import lax
from jax.experimental import pallas as pl
from jax.experimental.pallas import tpu as pltpu
from jax.sharding import PartitionSpec as P

HD = 128
FRAME_TOKENS = 3600
GRID_WIDTH = 80
ROWS = 16

X, Y, ZH, ZL, C = 4, 4, 2, 4, 2
J = 3

MARK = 16384.0
MARK_FLOOR = 1000.0
MARK_WEIGHT = -1048576.0
LOW = -1.0e30

K, KT, Q, QT, V, VT = range(6)
GROUPS = ((K, 1), (KT, 1), (Q, 2), (V, 1), (VT, 1))
GROUP_OF = {K: 0, KT: 1, Q: 2, V: 3, VT: 4}
RING = (K, KT, V, VT)
RELAYED = (KT,)


def device(x, y, z, c):
    return (y * (ZH * X) + lax.div(z, ZL) * X + x, lax.rem(z, ZL) * C + c)


def nt_dot(a, b):
    return lax.dot_general(a, b, (((1,), (1,)), ((), ())), preferred_element_type=jnp.float32)


def nn_dot(a, b):
    return jnp.dot(a, b, preferred_element_type=jnp.float32)


def kernel(
    q_in, k_in, v_in, qt_in, kt_in, vt_in, frame_in, count_in,
    o_out, ot_out,
    frame_ref, count_ref, raw, send, kv, s_ref, p_ref, w_ref,
    acc_p, acc_w, acc_t, mx, mx_late, alpha, lsum, gsum, outsend, passing,
    small, isem, dsem, rsem, ssem, dsend, rsend, bsend, osem, osend, psem, psend,
):
    Z = ZH * ZL
    heads = Z * J
    span = Z * ROWS
    chunks = X * C
    near = Z // 2
    rows = Y * span
    side = rows // 2
    scale = 1.0 / math.sqrt(HD)
    scale2 = scale * math.log2(math.e)

    blk = lax.axis_index("blk")
    hd = lax.axis_index("head")
    x = lax.rem(blk, X)
    y = lax.div(blk, ZH * X)
    z = lax.rem(lax.div(blk, X), ZH) * ZL + lax.div(hd, C)
    c = lax.rem(hd, C)
    right = device(lax.rem(x + 1, X), y, z, c)
    left = device(lax.rem(x + X - 1, X), y, z, c)
    sib = device(x, y, z, 1 - c)
    across_x = lax.rem(x + 2, X)
    relay = device(x, Y - 1, z, c)
    own = (x * C + c) * 2
    computes = y < J

    def fetch(ref, slot):
        return pltpu.make_async_copy(ref, raw.at[slot], isem.at[slot])

    frames_copy = pltpu.make_async_copy(frame_in, frame_ref, small.at[0])
    counts_copy = pltpu.make_async_copy(count_in, count_ref, small.at[1])
    frames_copy.start()
    counts_copy.start()
    fetch(k_in, K).start()

    barrier = pltpu.get_barrier_semaphore()

    def greet(i, carry):
        gz = lax.rem(z + near + i, Z)
        for gy in range(Y):

            @pl.when(jnp.logical_or(gy != y, gz != z))
            def _():
                pl.semaphore_signal(barrier, inc=1, device_id=device(x, gy, gz, c))

        return carry

    lax.fori_loop(0, Z, greet, 0)
    for other in (right, left, sib):
        pl.semaphore_signal(barrier, inc=1, device_id=other)

    @pl.when(computes)
    def _():
        pl.semaphore_signal(barrier, inc=1, device_id=device(across_x, Y - 1, z, c))

    @pl.when(jnp.logical_not(computes))
    def _():
        for j in range(J):
            pl.semaphore_signal(barrier, inc=1, device_id=device(across_x, j, z, c))


    for ref, slot in ((kt_in, KT), (q_in, Q), (qt_in, QT), (v_in, V), (vt_in, VT)):
        fetch(ref, slot).start()

    frames_copy.wait()
    counts_copy.wait()
    row = lax.broadcasted_iota(jnp.int32, (ROWS, HD), 0)
    lane = lax.broadcasted_iota(jnp.int32, (ROWS, HD), 1)
    frame = jnp.zeros((ROWS, HD), jnp.float32)
    for i in range(ROWS):
        frame = jnp.where(row == i, frame_ref[hd * ROWS + i].astype(jnp.float32), frame)
    valid = hd * ROWS + row < count_ref[0]
    token = blk * (ROWS * ZL * C) + hd * ROWS + row
    token = jnp.where(token >= FRAME_TOKENS, token - FRAME_TOKENS, token).astype(jnp.float32)
    height = jnp.floor((token + 0.5) * (1.0 / GRID_WIDTH))
    across = token - height * GRID_WIDTH
    pair = lax.rem(lane, HD // 2)
    spatial = HD // 6
    temporal = HD // 2 - 2 * spatial
    is_frame = pair < temporal
    is_height = pair < temporal + spatial
    index = jnp.where(is_frame, pair, jnp.where(is_height, pair - temporal, pair - temporal - spatial))
    count = jnp.where(is_frame, float(temporal), float(spatial))
    freqs = jnp.exp(-math.log(10000.0) * index.astype(jnp.float32) / count)
    angles = jnp.where(is_frame, frame, jnp.where(is_height, height, across)) * freqs
    cosine = jnp.cos(angles)
    sine = jnp.sin(angles)
    sine = jnp.where(lane < HD // 2, -sine, sine)

    def rotate(ref, slot, marked=False):
        fetch(ref, slot).wait()
        for h in range(heads):
            wide = raw[slot, :, h * HD : (h + 1) * HD].astype(jnp.float32)
            turned = wide * cosine + pltpu.roll(wide, HD // 2, 1) * sine
            if marked:
                turned = jnp.where(valid, turned, MARK)
            send[h, slot] = turned.astype(jnp.bfloat16)

    def place(ref, slot):
        fetch(ref, slot).wait()
        for h in range(heads):
            send[h, slot] = raw[slot, :, h * HD : (h + 1) * HD]

    def direct(a):
        g = GROUP_OF[a]
        first, count = GROUPS[g]

        def step(i, carry):
            tz = lax.rem(z + 2 + Z - i, Z)
            u = lax.div(i, near)
            slot = lax.rem(i, near)
            for j in range(J):
                src = send.at[tz * J + j, pl.ds(first, count)]
                dst = kv.at[pl.ds(first, count), own + u, y, pl.ds(slot * ROWS, ROWS)]
                here = jnp.logical_and(tz == z, y == j)

                @pl.when(here)
                def _():
                    pltpu.make_async_copy(src, dst, dsem.at[g, u]).start()

                @pl.when(jnp.logical_not(here))
                def _():
                    pltpu.make_async_remote_copy(
                        src_ref=src, dst_ref=dst, send_sem=dsend.at[g], recv_sem=dsem.at[g, u],
                        device_id=device(x, j, tz, c),
                    ).start()

            return carry

        lax.fori_loop(0, Z, step, 0)

    def wait_direct(a, u):
        g = GROUP_OF[a]
        first, count = GROUPS[g]
        region = kv.at[pl.ds(first, count), own + u]
        pltpu.make_async_copy(region, region, dsem.at[g, u]).wait()

    def ring_send(a, part, to, event):
        n = RING.index(a)
        pltpu.make_async_remote_copy(
            src_ref=part, dst_ref=part, send_sem=rsend.at[n], recv_sem=rsem.at[n, event],
            device_id=to,
        ).start()

    def sib_send(a, part, event):
        n = RING.index(a)
        pltpu.make_async_remote_copy(
            src_ref=part, dst_ref=part, send_sem=bsend.at[n], recv_sem=ssem.at[n, event],
            device_id=sib,
        ).start()

    def origin(i):
        step = jnp.where(lax.rem(i, 2) == 0, X - 1, 1)
        sx = lax.rem(x + jnp.where(i < 2, 0, jnp.where(i < 6, step, 2)), X)
        u = jnp.where(i < 2, i, jnp.where(i < 6, lax.div(i - 2, 2), i - 6))
        return sx, u

    def places(i):
        sx, u = origin(i)
        return (sx * C + c) * 2 + u, (sx * C + 1 - c) * 2 + u

    def start(a, u):
        wait_direct(a, u)
        part = kv.at[a, own + u]
        ring_send(a, part, right, u)
        ring_send(a, part, left, u)
        if a in RELAYED and u == 1:
            r = RELAYED.index(a)
            pltpu.make_async_remote_copy(
                src_ref=part, dst_ref=passing.at[r, y], send_sem=rsend.at[RING.index(a)],
                recv_sem=psem.at[r, y], device_id=relay,
            ).start()
        sib_send(a, part, 0)

    def arrived(sem, units_of):
        part = kv.at[0, pl.ds(0, units_of)]
        pltpu.make_async_copy(part, part, sem).wait()

    def unit_halves(a, i):
        place = places(jnp.int32(i))[0]
        half = Y // 2
        return kv.at[a, place], kv.at[a, place, pl.ds(0, half)], kv.at[a, place, pl.ds(half, half)]

    def neighbours(a, u):
        arrived(rsem.at[RING.index(a), u], 2)
        from_left, first, _ = unit_halves(a, 2 + 2 * u)
        from_right, _, second = unit_halves(a, 3 + 2 * u)
        if a not in RELAYED or u == 0:
            ring_send(a, first, right, 2 + u)
            ring_send(a, second, left, 2 + u)
        sib_send(a, from_left, 1 + u)
        sib_send(a, from_right, 1 + u)

    def opposite(a, u):
        arrived(rsem.at[RING.index(a), 2 + u], 1)
        sib_send(a, unit_halves(a, 6 + u)[0], 3)

    def wait_sibs(a, j):
        arrived(ssem.at[RING.index(a), j], 2)

    def queries_of(a):
        return kv[a, pl.ds(own, 2)].reshape(rows, HD)

    def units(a, j):
        parts = []
        for n in range(2):
            for place in places(2 * j + n):
                parts.append(kv[a, place].reshape(side, HD))
        return parts

    def lanes(op, total, array):
        for t in range(array.shape[1] // HD):
            total = op(total, array[:, t * HD : (t + 1) * HD])
        return total

    def scores(j, top):
        wait_sibs(K, j)
        keys = units(K, j)
        last = side // Y
        marks = []
        for part in keys:
            over = jnp.maximum(part[side - last :].astype(jnp.float32) - MARK_FLOOR, 0.0)
            marks.append(jnp.zeros((side - last, HD), jnp.bfloat16))
            marks.append(over.astype(jnp.bfloat16))
        weight = jnp.full((rows, HD), MARK_WEIGHT, jnp.bfloat16)
        s = nt_dot(
            jnp.concatenate([queries_of(Q), weight], axis=1),
            jnp.concatenate([jnp.concatenate(keys, axis=0), jnp.concatenate(marks, axis=0)], axis=1),
        )
        s_ref[j] = s
        top[...] = lanes(jnp.maximum, top[...], s)

    def weights(j, top):
        wait_sibs(KT, j)
        top = jnp.concatenate([top[...]] * (2 * rows // HD), axis=1)
        p = jnp.exp2(s_ref[j] * scale2 - top)
        g = nt_dot(
            jnp.concatenate([queries_of(QT), queries_of(Q)], axis=1),
            jnp.concatenate(
                [jnp.concatenate(units(K, j), axis=0), jnp.concatenate(units(KT, j), axis=0)], axis=1
            ),
        )
        w = p * g
        lsum[...] = lanes(jnp.add, lsum[...], p)
        gsum[...] = lanes(jnp.add, gsum[...], w)
        p_ref[j] = p.astype(jnp.bfloat16)
        w_ref[j] = w.astype(jnp.bfloat16)

    def stacked(a, steps):
        parts = []
        for j in steps:
            wait_sibs(a, j)
        for j in steps:
            parts += units(a, j)
        return jnp.concatenate(parts, axis=0)

    def product(ref, steps, right_side, part=slice(None)):
        return nn_dot(jnp.concatenate([ref[j, part] for j in steps], axis=1), right_side)

    def give(which, u):
        out = (o_out, ot_out)[which]

        def step(k, carry):
            tz = lax.rem(z + u * near + k + Z - 2, Z)
            for ty in range(Y):
                src = outsend.at[which, (u * Y + ty) * near + k]
                dst = out.at[:, pl.ds(pl.multiple_of((z * J + y) * HD, HD), HD)]
                here = jnp.logical_and(tz == z, y == ty)

                @pl.when(here)
                def _():
                    pltpu.make_async_copy(src, dst, osem.at[which]).start()

                @pl.when(jnp.logical_not(here))
                def _():
                    pltpu.make_async_remote_copy(
                        src_ref=src, dst_ref=dst, send_sem=osend.at[which],
                        recv_sem=osem.at[which], device_id=device(x, ty, tz, c),
                    ).start()

            return carry

        lax.fori_loop(0, near, step, 0)

    def loop(work, low, high, beside=None):
        def step(i, carry):
            for k, act in (beside or {}).items():
                pl.when(i == k)(act)
            work(i)
            return carry

        lax.fori_loop(low, high, step, 0)

    rotate(k_in, K, True)
    pl.semaphore_wait(barrier, Y * Z - 1 + 3 + jnp.where(computes, 1, J))
    direct(K)
    rotate(kt_in, KT)
    direct(KT)
    rotate(q_in, Q)
    rotate(qt_in, QT)
    direct(Q)
    place(v_in, V)
    direct(V)
    place(vt_in, VT)
    direct(VT)

    @pl.when(computes)
    def _():
        start(K, 0)
        mx[...] = jnp.full_like(mx, LOW)
        mx_late[...] = jnp.full_like(mx, LOW)
        lsum[...] = jnp.zeros_like(lsum)
        gsum[...] = jnp.zeros_like(gsum)
        start(K, 1)
        start(KT, 0)
        start(KT, 1)
        neighbours(K, 0)
        neighbours(K, 1)
        wait_direct(Q, 0)
        wait_direct(Q, 1)
        loop(lambda j: scores(j, mx), 0, 3, {
            1: lambda: neighbours(KT, 0),
            2: lambda: start(V, 0),
        })
        opposite(K, 0)
        start(V, 1)
        neighbours(KT, 1)
        mx[...] = jnp.broadcast_to(jnp.max(mx[...], axis=1, keepdims=True) * scale2, mx.shape)
        opposite(K, 1)

        loop(lambda j: weights(j, mx), 0, 3, {
            1: lambda: start(VT, 0),
            2: lambda: start(VT, 1),
        })
        opposite(KT, 0)
        scores(3, mx_late)
        neighbours(V, 0)
        opposite(KT, 1)
        neighbours(V, 1)
        early, middle, late = range(2), range(2, 3), range(3, 4)
        v = stacked(V, early)
        acc_p[...] = product(p_ref, early, v)
        acc_w[...] = product(w_ref, early, v)
        neighbours(VT, 0)
        top = jnp.maximum(mx[...], jnp.max(mx_late[...], axis=1, keepdims=True) * scale2)
        factor = jnp.exp2(mx[...] - top)
        alpha[...] = factor
        mx[...] = top
        lsum[...] = lsum[...] * factor
        gsum[...] = gsum[...] * factor
        weights(3, mx)
        neighbours(VT, 1)
        v = stacked(V, middle)
        acc_p[...] += product(p_ref, middle, v)
        acc_w[...] += product(w_ref, middle, v)
        opposite(V, 0)
        acc_t[...] = product(p_ref, early, stacked(VT, early))
        opposite(V, 1)
        acc_t[...] += product(p_ref, middle, stacked(VT, middle))
        v = stacked(V, late)
        inverse = 1.0 / jnp.sum(lsum[...], axis=1, keepdims=True)
        slope = jnp.sum(gsum[...], axis=1, keepdims=True) * inverse * scale
        attended = (acc_p[...] * alpha[...] + product(p_ref, late, v)) * inverse
        outsend[0] = attended.astype(jnp.bfloat16).reshape(Y * Z, ROWS, HD)
        give(0, 1)
        give(0, 0)
        opposite(VT, 0)
        opposite(VT, 1)
        acc_w[...] = (acc_w[...] * alpha[...] + product(w_ref, late, v)) * (
            inverse * scale
        ) - slope * attended
        lsum[...] = jnp.broadcast_to(inverse, lsum.shape)
        acc_t[...] = acc_t[...] * (alpha[...] * lsum[...]) + acc_w[...]
        v = stacked(VT, late)
        for u in (1, 0):
            part = slice(u * side, (u + 1) * side)
            tangent = acc_t[part] + product(p_ref, late, v, part) * lsum[part]
            outsend[1, u * Y * near : (u + 1) * Y * near] = tangent.astype(
                jnp.bfloat16
            ).reshape(Y * near, ROWS, HD)
            give(1, u)

    @pl.when(jnp.logical_not(computes))
    def _():
        for r, a in enumerate(RELAYED):
            for j in range(J):
                part = passing.at[r, j]
                pltpu.make_async_copy(part, part, psem.at[r, j]).wait()
                pltpu.make_async_remote_copy(
                    src_ref=part, dst_ref=kv.at[a, own + 1], send_sem=psend,
                    recv_sem=rsem.at[RING.index(a), 3], device_id=device(across_x, j, z, c),
                ).start()

    def sent(count):
        for g, (first, arrays) in enumerate(GROUPS):
            part = send.at[pl.ds(0, count), pl.ds(first, arrays)]
            pltpu.make_async_copy(part, part, dsend.at[g]).wait()

    @pl.when(computes)
    def _():
        sent(heads - 1)
        for n in range(4):
            part = kv.at[0, pl.ds(0, 6)]
            pltpu.make_async_copy(part, part, rsend.at[n]).wait()
            part = kv.at[0, pl.ds(0, 8)]
            pltpu.make_async_copy(part, part, bsend.at[n]).wait()
        for which in range(2):
            part = outsend.at[which, pl.ds(0, Y * Z - 1)]
            pltpu.make_async_copy(part, part, osend.at[which]).wait()

    @pl.when(jnp.logical_not(computes))
    def _():
        sent(heads)
        arrived(psend, len(RELAYED) * J)

    for which, out in ((0, o_out), (1, ot_out)):
        pltpu.make_async_copy(out, out, osem.at[which]).wait()


def shards(queries, key_vectors, values, query_tangent, key_tangent, value_tangent,
           frame_index, valid_counts):
    Z = ZH * ZL
    heads = Z * J
    span = Z * ROWS
    rows = Y * span
    chunks = X * C
    hbm = pl.BlockSpec(memory_space=pl.ANY)
    out = jax.ShapeDtypeStruct((ROWS, heads * HD), jnp.bfloat16)
    return pl.pallas_call(
        kernel,
        out_shape=(out, out),
        in_specs=[hbm] * 8,
        out_specs=(hbm, hbm),
        scratch_shapes=[
            pltpu.SMEM((ROWS * ZL * C,), jnp.int32),
            pltpu.SMEM((1,), jnp.int32),
            pltpu.VMEM((6, ROWS, heads * HD), jnp.bfloat16),
            pltpu.VMEM((heads, 6, ROWS, HD), jnp.bfloat16),
            pltpu.VMEM((6, chunks * 2, Y, span // 2, HD), jnp.bfloat16),
            pltpu.VMEM((chunks // 2, rows, 2 * rows), jnp.float32),
            pltpu.VMEM((chunks // 2, rows, 2 * rows), jnp.bfloat16),
            pltpu.VMEM((chunks // 2, rows, 2 * rows), jnp.bfloat16),
            pltpu.VMEM((rows, HD), jnp.float32),
            pltpu.VMEM((rows, HD), jnp.float32),
            pltpu.VMEM((rows, HD), jnp.float32),
            pltpu.VMEM((rows, HD), jnp.float32),
            pltpu.VMEM((rows, HD), jnp.float32),
            pltpu.VMEM((rows, HD), jnp.float32),
            pltpu.VMEM((rows, HD), jnp.float32),
            pltpu.VMEM((rows, HD), jnp.float32),
            pltpu.VMEM((2, Y * Z, ROWS, HD), jnp.bfloat16),
            pltpu.VMEM((len(RELAYED), J, Y, span // 2, HD), jnp.bfloat16),
            pltpu.SemaphoreType.DMA((2,)),
            pltpu.SemaphoreType.DMA((6,)),
            pltpu.SemaphoreType.DMA((5, 2)),
            pltpu.SemaphoreType.DMA((4, 4)),
            pltpu.SemaphoreType.DMA((4, 4)),
            pltpu.SemaphoreType.DMA((5,)),
            pltpu.SemaphoreType.DMA((4,)),
            pltpu.SemaphoreType.DMA((4,)),
            pltpu.SemaphoreType.DMA((2,)),
            pltpu.SemaphoreType.DMA((2,)),
            pltpu.SemaphoreType.DMA((len(RELAYED), J)),
            pltpu.SemaphoreType.DMA,
        ],
        compiler_params=pltpu.CompilerParams(
            collective_id=0, has_side_effects=True, vmem_limit_bytes=54975 * 1024
        ),
    )(queries, key_vectors, values, query_tangent, key_tangent, value_tangent,
      frame_index, valid_counts)


def solution(mesh):
    tokens = P(("blk", "head"), None)
    return jax.shard_map(
        shards,
        mesh=mesh,
        in_specs=(tokens,) * 6 + (P("blk"), P("blk")),
        out_specs=(tokens, tokens),
        check_vma=False,
    )
```

```python
import math

import jax
import jax.numpy as jnp
from jax import lax
from jax.experimental import pallas as pl
from jax.experimental.pallas import tpu as pltpu
from jax.sharding import PartitionSpec as P

HD = 128
FRAME_TOKENS = 3600
GRID_WIDTH = 80
ROWS = 16

X, Y, ZH, ZL, C = 4, 4, 2, 4, 2
J = 3

MARK = 16384.0
MARK_FLOOR = 1000.0
MARK_WEIGHT = -1048576.0
LOW = -1.0e30

K, KT, Q, QT, V, VT = range(6)
GROUPS = ((K, 1), (KT, 1), (Q, 2), (V, 1), (VT, 1))
GROUP_OF = {K: 0, KT: 1, Q: 2, V: 3, VT: 4}
RING = (K, KT, V, VT)
RELAYED = (KT,)


def device(x, y, z, c):
    return (y * (ZH * X) + lax.div(z, ZL) * X + x, lax.rem(z, ZL) * C + c)


def nt_dot(a, b):
    return lax.dot_general(a, b, (((1,), (1,)), ((), ())), preferred_element_type=jnp.float32)


def nn_dot(a, b):
    return jnp.dot(a, b, preferred_element_type=jnp.float32)


def kernel(
    q_in, k_in, v_in, qt_in, kt_in, vt_in, frame_in, count_in,
    o_out, ot_out,
    frame_ref, count_ref, raw, send, kv, s_ref, p_ref, w_ref,
    acc_p, acc_w, acc_t, mx, mx_late, alpha, lsum, gsum, outsend, passing,
    small, isem, dsem, rsem, ssem, dsend, rsend, bsend, osem, osend, psem, psend,
):
    Z = ZH * ZL
    heads = Z * J
    span = Z * ROWS
    chunks = X * C
    near = Z // 2
    rows = Y * span
    side = rows // 2
    scale = 1.0 / math.sqrt(HD)
    scale2 = scale * math.log2(math.e)

    blk = lax.axis_index("blk")
    hd = lax.axis_index("head")
    x = lax.rem(blk, X)
    y = lax.div(blk, ZH * X)
    z = lax.rem(lax.div(blk, X), ZH) * ZL + lax.div(hd, C)
    c = lax.rem(hd, C)
    right = device(lax.rem(x + 1, X), y, z, c)
    left = device(lax.rem(x + X - 1, X), y, z, c)
    sib = device(x, y, z, 1 - c)
    across_x = lax.rem(x + 2, X)
    relay = device(x, Y - 1, z, c)
    own = (x * C + c) * 2
    computes = y < J

    def fetch(ref, slot):
        return pltpu.make_async_copy(ref, raw.at[slot], isem.at[slot])

    frames_copy = pltpu.make_async_copy(frame_in, frame_ref, small.at[0])
    counts_copy = pltpu.make_async_copy(count_in, count_ref, small.at[1])
    frames_copy.start()
    counts_copy.start()
    fetch(k_in, K).start()

    barrier = pltpu.get_barrier_semaphore()

    def greet(i, carry):
        gz = lax.rem(z + near + i, Z)
        for gy in range(Y):

            @pl.when(jnp.logical_or(gy != y, gz != z))
            def _():
                pl.semaphore_signal(barrier, inc=1, device_id=device(x, gy, gz, c))

        return carry

    lax.fori_loop(0, Z, greet, 0)
    for other in (right, left, sib):
        pl.semaphore_signal(barrier, inc=1, device_id=other)

    @pl.when(computes)
    def _():
        pl.semaphore_signal(barrier, inc=1, device_id=device(across_x, Y - 1, z, c))

    @pl.when(jnp.logical_not(computes))
    def _():
        for j in range(J):
            pl.semaphore_signal(barrier, inc=1, device_id=device(across_x, j, z, c))


    for ref, slot in ((kt_in, KT), (q_in, Q), (qt_in, QT), (v_in, V), (vt_in, VT)):
        fetch(ref, slot).start()

    frames_copy.wait()
    counts_copy.wait()
    row = lax.broadcasted_iota(jnp.int32, (ROWS, HD), 0)
    lane = lax.broadcasted_iota(jnp.int32, (ROWS, HD), 1)
    frame = jnp.zeros((ROWS, HD), jnp.float32)
    for i in range(ROWS):
        frame = jnp.where(row == i, frame_ref[hd * ROWS + i].astype(jnp.float32), frame)
    valid = hd * ROWS + row < count_ref[0]
    token = blk * (ROWS * ZL * C) + hd * ROWS + row
    token = jnp.where(token >= FRAME_TOKENS, token - FRAME_TOKENS, token).astype(jnp.float32)
    height = jnp.floor((token + 0.5) * (1.0 / GRID_WIDTH))
    across = token - height * GRID_WIDTH
    pair = lax.rem(lane, HD // 2)
    spatial = HD // 6
    temporal = HD // 2 - 2 * spatial
    is_frame = pair < temporal
    is_height = pair < temporal + spatial
    index = jnp.where(is_frame, pair, jnp.where(is_height, pair - temporal, pair - temporal - spatial))
    count = jnp.where(is_frame, float(temporal), float(spatial))
    freqs = jnp.exp(-math.log(10000.0) * index.astype(jnp.float32) / count)
    angles = jnp.where(is_frame, frame, jnp.where(is_height, height, across)) * freqs
    cosine = jnp.cos(angles)
    sine = jnp.sin(angles)
    sine = jnp.where(lane < HD // 2, -sine, sine)

    def rotate(ref, slot, marked=False):
        fetch(ref, slot).wait()
        for h in range(heads):
            wide = raw[slot, :, h * HD : (h + 1) * HD].astype(jnp.float32)
            turned = wide * cosine + pltpu.roll(wide, HD // 2, 1) * sine
            if marked:
                turned = jnp.where(valid, turned, MARK)
            send[h, slot] = turned.astype(jnp.bfloat16)

    def place(ref, slot):
        fetch(ref, slot).wait()
        for h in range(heads):
            send[h, slot] = raw[slot, :, h * HD : (h + 1) * HD]

    def direct(a):
        g = GROUP_OF[a]
        first, count = GROUPS[g]

        def step(i, carry):
            tz = lax.rem(z + 2 + Z - i, Z)
            u = lax.div(i, near)
            slot = lax.rem(i, near)
            for j in range(J):
                src = send.at[tz * J + j, pl.ds(first, count)]
                dst = kv.at[pl.ds(first, count), own + u, y, pl.ds(slot * ROWS, ROWS)]
                here = jnp.logical_and(tz == z, y == j)

                @pl.when(here)
                def _():
                    pltpu.make_async_copy(src, dst, dsem.at[g, u]).start()

                @pl.when(jnp.logical_not(here))
                def _():
                    pltpu.make_async_remote_copy(
                        src_ref=src, dst_ref=dst, send_sem=dsend.at[g], recv_sem=dsem.at[g, u],
                        device_id=device(x, j, tz, c),
                    ).start()

            return carry

        lax.fori_loop(0, Z, step, 0)

    def wait_direct(a, u):
        g = GROUP_OF[a]
        first, count = GROUPS[g]
        region = kv.at[pl.ds(first, count), own + u]
        pltpu.make_async_copy(region, region, dsem.at[g, u]).wait()

    def ring_send(a, part, to, event):
        n = RING.index(a)
        pltpu.make_async_remote_copy(
            src_ref=part, dst_ref=part, send_sem=rsend.at[n], recv_sem=rsem.at[n, event],
            device_id=to,
        ).start()

    def sib_send(a, part, event):
        n = RING.index(a)
        pltpu.make_async_remote_copy(
            src_ref=part, dst_ref=part, send_sem=bsend.at[n], recv_sem=ssem.at[n, event],
            device_id=sib,
        ).start()

    def origin(i):
        step = jnp.where(lax.rem(i, 2) == 0, X - 1, 1)
        sx = lax.rem(x + jnp.where(i < 2, 0, jnp.where(i < 6, step, 2)), X)
        u = jnp.where(i < 2, i, jnp.where(i < 6, lax.div(i - 2, 2), i - 6))
        return sx, u

    def places(i):
        sx, u = origin(i)
        return (sx * C + c) * 2 + u, (sx * C + 1 - c) * 2 + u

    def start(a, u):
        wait_direct(a, u)
        part = kv.at[a, own + u]
        ring_send(a, part, right, u)
        ring_send(a, part, left, u)
        if a in RELAYED and u == 1:
            r = RELAYED.index(a)
            pltpu.make_async_remote_copy(
                src_ref=part, dst_ref=passing.at[r, y], send_sem=rsend.at[RING.index(a)],
                recv_sem=psem.at[r, y], device_id=relay,
            ).start()
        sib_send(a, part, 0)

    def arrived(sem, units_of):
        part = kv.at[0, pl.ds(0, units_of)]
        pltpu.make_async_copy(part, part, sem).wait()

    def unit_halves(a, i):
        place = places(jnp.int32(i))[0]
        half = Y // 2
        return kv.at[a, place], kv.at[a, place, pl.ds(0, half)], kv.at[a, place, pl.ds(half, half)]

    def neighbours(a, u):
        arrived(rsem.at[RING.index(a), u], 2)
        from_left, first, _ = unit_halves(a, 2 + 2 * u)
        from_right, _, second = unit_halves(a, 3 + 2 * u)
        if a not in RELAYED or u == 0:
            ring_send(a, first, right, 2 + u)
            ring_send(a, second, left, 2 + u)
        sib_send(a, from_left, 1 + u)
        sib_send(a, from_right, 1 + u)

    def opposite(a, u):
        arrived(rsem.at[RING.index(a), 2 + u], 1)
        sib_send(a, unit_halves(a, 6 + u)[0], 3)

    def wait_sibs(a, j):
        arrived(ssem.at[RING.index(a), j], 2)

    def queries_of(a):
        return kv[a, pl.ds(own, 2)].reshape(rows, HD)

    def units(a, j):
        parts = []
        for n in range(2):
            for place in places(2 * j + n):
                parts.append(kv[a, place].reshape(side, HD))
        return parts

    def lanes(op, total, array):
        for t in range(array.shape[1] // HD):
            total = op(total, array[:, t * HD : (t + 1) * HD])
        return total

    def scores(j, top):
        wait_sibs(K, j)
        keys = units(K, j)
        last = side // Y
        marks = []
        for part in keys:
            over = jnp.maximum(part[side - last :].astype(jnp.float32) - MARK_FLOOR, 0.0)
            marks.append(jnp.zeros((side - last, HD), jnp.bfloat16))
            marks.append(over.astype(jnp.bfloat16))
        weight = jnp.full((rows, HD), MARK_WEIGHT, jnp.bfloat16)
        s = nt_dot(
            jnp.concatenate([queries_of(Q), weight], axis=1),
            jnp.concatenate([jnp.concatenate(keys, axis=0), jnp.concatenate(marks, axis=0)], axis=1),
        )
        s_ref[j] = s
        top[...] = lanes(jnp.maximum, top[...], s)

    def weights(j, top):
        wait_sibs(KT, j)
        top = jnp.concatenate([top[...]] * (2 * rows // HD), axis=1)
        p = jnp.exp2(s_ref[j] * scale2 - top)
        g = nt_dot(
            jnp.concatenate([queries_of(QT), queries_of(Q)], axis=1),
            jnp.concatenate(
                [jnp.concatenate(units(K, j), axis=0), jnp.concatenate(units(KT, j), axis=0)], axis=1
            ),
        )
        w = p * g
        lsum[...] = lanes(jnp.add, lsum[...], p)
        gsum[...] = lanes(jnp.add, gsum[...], w)
        p_ref[j] = p.astype(jnp.bfloat16)
        w_ref[j] = w.astype(jnp.bfloat16)

    def stacked(a, steps):
        parts = []
        for j in steps:
            wait_sibs(a, j)
        for j in steps:
            parts += units(a, j)
        return jnp.concatenate(parts, axis=0)

    def product(ref, steps, right_side, part=slice(None)):
        return nn_dot(jnp.concatenate([ref[j, part] for j in steps], axis=1), right_side)

    def give(which, u):
        out = (o_out, ot_out)[which]

        def step(k, carry):
            tz = lax.rem(z + u * near + k + Z - 2, Z)
            for ty in range(Y):
                src = outsend.at[which, (u * Y + ty) * near + k]
                dst = out.at[:, pl.ds(pl.multiple_of((z * J + y) * HD, HD), HD)]
                here = jnp.logical_and(tz == z, y == ty)

                @pl.when(here)
                def _():
                    pltpu.make_async_copy(src, dst, osem.at[which]).start()

                @pl.when(jnp.logical_not(here))
                def _():
                    pltpu.make_async_remote_copy(
                        src_ref=src, dst_ref=dst, send_sem=osend.at[which],
                        recv_sem=osem.at[which], device_id=device(x, ty, tz, c),
                    ).start()

            return carry

        lax.fori_loop(0, near, step, 0)

    def loop(work, low, high, beside=None):
        def step(i, carry):
            for k, act in (beside or {}).items():
                pl.when(i == k)(act)
            work(i)
            return carry

        lax.fori_loop(low, high, step, 0)

    rotate(k_in, K, True)
    pl.semaphore_wait(barrier, Y * Z - 1 + 3 + jnp.where(computes, 1, J))
    direct(K)
    rotate(kt_in, KT)
    direct(KT)
    rotate(q_in, Q)
    rotate(qt_in, QT)
    direct(Q)
    place(v_in, V)
    direct(V)
    place(vt_in, VT)
    direct(VT)

    @pl.when(computes)
    def _():
        start(K, 0)
        mx[...] = jnp.full_like(mx, LOW)
        mx_late[...] = jnp.full_like(mx, LOW)
        lsum[...] = jnp.zeros_like(lsum)
        gsum[...] = jnp.zeros_like(gsum)
        start(K, 1)
        start(KT, 0)
        start(KT, 1)
        neighbours(K, 0)
        neighbours(K, 1)
        wait_direct(Q, 0)
        wait_direct(Q, 1)
        loop(lambda j: scores(j, mx), 0, 3, {
            1: lambda: neighbours(KT, 0),
            2: lambda: start(V, 0),
        })
        opposite(K, 0)
        start(V, 1)
        neighbours(KT, 1)
        mx[...] = jnp.broadcast_to(jnp.max(mx[...], axis=1, keepdims=True) * scale2, mx.shape)
        opposite(K, 1)

        def second():
            start(VT, 0)
            opposite(KT, 0)

        def third():
            start(VT, 1)
            neighbours(V, 0)

        loop(lambda j: weights(j, mx), 0, 3, {1: second, 2: third})
        scores(3, mx_late)
        opposite(KT, 1)
        neighbours(V, 1)
        early, middle, late = range(2), range(2, 3), range(3, 4)
        v = stacked(V, early)
        acc_p[...] = product(p_ref, early, v)
        acc_w[...] = product(w_ref, early, v)
        neighbours(VT, 0)
        top = jnp.maximum(mx[...], jnp.max(mx_late[...], axis=1, keepdims=True) * scale2)
        factor = jnp.exp2(mx[...] - top)
        alpha[...] = factor
        mx[...] = top
        lsum[...] = lsum[...] * factor
        gsum[...] = gsum[...] * factor
        weights(3, mx)
        neighbours(VT, 1)
        v = stacked(V, middle)
        acc_p[...] += product(p_ref, middle, v)
        acc_w[...] += product(w_ref, middle, v)
        opposite(V, 0)
        acc_t[...] = product(p_ref, early, stacked(VT, early))
        opposite(V, 1)
        acc_t[...] += product(p_ref, middle, stacked(VT, middle))
        v = stacked(V, late)
        inverse = 1.0 / jnp.sum(lsum[...], axis=1, keepdims=True)
        slope = jnp.sum(gsum[...], axis=1, keepdims=True) * inverse * scale
        attended = (acc_p[...] * alpha[...] + product(p_ref, late, v)) * inverse
        outsend[0] = attended.astype(jnp.bfloat16).reshape(Y * Z, ROWS, HD)
        give(0, 1)
        opposite(VT, 0)
        opposite(VT, 1)
        give(0, 0)
        acc_w[...] = (acc_w[...] * alpha[...] + product(w_ref, late, v)) * (
            inverse * scale
        ) - slope * attended
        lsum[...] = jnp.broadcast_to(inverse, lsum.shape)
        acc_t[...] = acc_t[...] * (alpha[...] * lsum[...]) + acc_w[...]
        v = stacked(VT, late)
        for u in (1, 0):
            part = slice(u * side, (u + 1) * side)
            tangent = acc_t[part] + product(p_ref, late, v, part) * lsum[part]
            outsend[1, u * Y * near : (u + 1) * Y * near] = tangent.astype(
                jnp.bfloat16
            ).reshape(Y * near, ROWS, HD)
            give(1, u)

    @pl.when(jnp.logical_not(computes))
    def _():
        for r, a in enumerate(RELAYED):
            for j in range(J):
                part = passing.at[r, j]
                pltpu.make_async_copy(part, part, psem.at[r, j]).wait()
                pltpu.make_async_remote_copy(
                    src_ref=part, dst_ref=kv.at[a, own + 1], send_sem=psend,
                    recv_sem=rsem.at[RING.index(a), 3], device_id=device(across_x, j, z, c),
                ).start()

    for which, out in ((0, o_out), (1, ot_out)):
        pltpu.make_async_copy(out, out, osem.at[which]).wait()

    def sent(count):
        for g, (first, arrays) in enumerate(GROUPS):
            part = send.at[pl.ds(0, count), pl.ds(first, arrays)]
            pltpu.make_async_copy(part, part, dsend.at[g]).wait()

    @pl.when(computes)
    def _():
        sent(heads - 1)
        for n in range(4):
            part = kv.at[0, pl.ds(0, 6)]
            pltpu.make_async_copy(part, part, rsend.at[n]).wait()
            part = kv.at[0, pl.ds(0, 8)]
            pltpu.make_async_copy(part, part, bsend.at[n]).wait()
        for which in range(2):
            part = outsend.at[which, pl.ds(0, Y * Z - 1)]
            pltpu.make_async_copy(part, part, osend.at[which]).wait()

    @pl.when(jnp.logical_not(computes))
    def _():
        sent(heads)
        arrived(psend, len(RELAYED) * J)


def shards(queries, key_vectors, values, query_tangent, key_tangent, value_tangent,
           frame_index, valid_counts):
    Z = ZH * ZL
    heads = Z * J
    span = Z * ROWS
    rows = Y * span
    chunks = X * C
    hbm = pl.BlockSpec(memory_space=pl.ANY)
    out = jax.ShapeDtypeStruct((ROWS, heads * HD), jnp.bfloat16)
    return pl.pallas_call(
        kernel,
        out_shape=(out, out),
        in_specs=[hbm] * 8,
        out_specs=(hbm, hbm),
        scratch_shapes=[
            pltpu.SMEM((ROWS * ZL * C,), jnp.int32),
            pltpu.SMEM((1,), jnp.int32),
            pltpu.VMEM((6, ROWS, heads * HD), jnp.bfloat16),
            pltpu.VMEM((heads, 6, ROWS, HD), jnp.bfloat16),
            pltpu.VMEM((6, chunks * 2, Y, span // 2, HD), jnp.bfloat16),
            pltpu.VMEM((chunks // 2, rows, 2 * rows), jnp.float32),
            pltpu.VMEM((chunks // 2, rows, 2 * rows), jnp.bfloat16),
            pltpu.VMEM((chunks // 2, rows, 2 * rows), jnp.bfloat16),
            pltpu.VMEM((rows, HD), jnp.float32),
            pltpu.VMEM((rows, HD), jnp.float32),
            pltpu.VMEM((rows, HD), jnp.float32),
            pltpu.VMEM((rows, HD), jnp.float32),
            pltpu.VMEM((rows, HD), jnp.float32),
            pltpu.VMEM((rows, HD), jnp.float32),
            pltpu.VMEM((rows, HD), jnp.float32),
            pltpu.VMEM((rows, HD), jnp.float32),
            pltpu.VMEM((2, Y * Z, ROWS, HD), jnp.bfloat16),
            pltpu.VMEM((len(RELAYED), J, Y, span // 2, HD), jnp.bfloat16),
            pltpu.SemaphoreType.DMA((2,)),
            pltpu.SemaphoreType.DMA((6,)),
            pltpu.SemaphoreType.DMA((5, 2)),
            pltpu.SemaphoreType.DMA((4, 4)),
            pltpu.SemaphoreType.DMA((4, 4)),
            pltpu.SemaphoreType.DMA((5,)),
            pltpu.SemaphoreType.DMA((4,)),
            pltpu.SemaphoreType.DMA((4,)),
            pltpu.SemaphoreType.DMA((2,)),
            pltpu.SemaphoreType.DMA((2,)),
            pltpu.SemaphoreType.DMA((len(RELAYED), J)),
            pltpu.SemaphoreType.DMA,
        ],
        compiler_params=pltpu.CompilerParams(
            collective_id=0, has_side_effects=True, vmem_limit_bytes=54975 * 1024
        ),
    )(queries, key_vectors, values, query_tangent, key_tangent, value_tangent,
      frame_index, valid_counts)


def solution(mesh):
    tokens = P(("blk", "head"), None)
    return jax.shard_map(
        shards,
        mesh=mesh,
        in_specs=(tokens,) * 6 + (P("blk"), P("blk")),
        out_specs=(tokens, tokens),
        check_vma=False,
    )
```
